128 devices in a mesh: src: 4 (over x), own: 32 (over y, z, core).
Axes of the slice: x: 4, y: 4, z: 4, core: 2. Of those that a mesh axis runs over, the one named last changes fastest.
Arguments:
- embeddings: bfloat16 [24576, 1024], P(('src', 'own'))
- cluster_ids: int32 [24576], P(('src', 'own')), may hold values from 0 to 1023, as said below
Outputs:
- best_similarity: float32 [24576], P(('src', 'own'))
The draws below stay inside these ranges and needn't reach their ends.
Inputs may be any that keep to these rules, and one draw needn't show every extreme that they name: A document's owner shard is cluster_ids // 32. Among the rows of one device at most 12 have one owner shard, and in every draw one owner shard gets exactly 12 rows from every device.
All inputs are finite; a program needn't handle non-finite values.
Results may differ from the reference program's by a relative error of at most 0.00037.
Values may be sent and summed in bfloat16 or wider, within the bound.
A program may use at most 64 MiB of HBM per device.

```python
import math
import jax
import jax.numpy as jnp
from jax import lax

D = 1024
DOC_DEV = 192
CL_OWN = 32
CAP = 12
CLUSTERS = 1024
DOCS = 24576
N_SRC = 4
N_OWN = 32


def cluster_layout(key):
    blocks = DOCS // DOC_DEV
    hottest = jax.random.randint(jax.random.fold_in(key, 11), (), 0, N_OWN)

    def one_block(block_key):
        keys = jax.random.split(block_key, 3)
        others = jnp.arange((N_OWN - 1) * CAP, dtype=jnp.int32) // CAP
        others = others + (others >= hottest).astype(jnp.int32)
        picked = jax.random.permutation(keys[0], others)[:DOC_DEV - CAP]
        owners = jnp.concatenate([jnp.full((CAP,), hottest, jnp.int32), picked])
        owners = jax.random.permutation(keys[1], owners)
        ranks = jnp.min(jax.random.randint(keys[2], (3, DOC_DEV), 0, CL_OWN), axis=0)
        return (owners, ranks)
    owners, ranks = jax.vmap(one_block)(jax.random.split(jax.random.fold_in(key, 12), blocks))
    shifts = jax.random.randint(jax.random.fold_in(key, 13), (N_OWN,), 0, CL_OWN)
    local = (ranks + shifts[owners]) % CL_OWN
    return (owners * CL_OWN + local).reshape(-1).astype(jnp.int32)


def draw_cluster_ids(key, part):
    return cluster_layout(key)


def pair_layout(clusters, chooser_key):
    order = jnp.argsort(clusters, stable=True).astype(jnp.int32)
    sorted_clusters = clusters[order]
    position = jnp.arange(DOCS, dtype=jnp.int32)
    cluster_start = jnp.concatenate([jnp.ones((1,), jnp.bool_), sorted_clusters[1:] != sorted_clusters[:-1]])
    first_place = lax.cummax(jnp.where(cluster_start, position, 0), axis=0)
    cluster_rank = position - first_place
    chosen = jax.random.randint(chooser_key, (DOCS,), 0, 10) == 0
    duplicate_sorted = (cluster_rank % 2 == 1) & chosen
    partner_sorted = order[jnp.maximum(position - 1, 0)]
    duplicate = jnp.zeros((DOCS,), jnp.bool_).at[order].set(duplicate_sorted)
    partner = jnp.zeros((DOCS,), jnp.int32).at[order].set(partner_sorted)
    marked = jnp.zeros((DOCS,), jnp.int32).at[partner].add(duplicate.astype(jnp.int32)) > 0
    return (duplicate, partner, duplicate | marked)


def draw_embeddings(key, part):
    clusters = cluster_layout(key)
    key = jax.random.fold_in(key, 5)
    keys = jax.random.split(key, 6)
    centroid = jax.random.normal(keys[0], (CLUSTERS, D), jnp.float32)
    noise = jax.random.normal(keys[1], (DOCS, D), jnp.float32)
    spread = jnp.exp(jax.random.uniform(keys[2], (DOCS, 1), jnp.float32, jnp.log(0.4), jnp.log(2.0)))
    widest = 2.0
    duplicate, partner, linked = pair_layout(clusters, keys[4])
    jitter = jax.random.normal(keys[5], (DOCS, D), jnp.float32)
    spread = jnp.where(linked[:, None], jnp.float32(widest), spread)
    noise = jnp.where(duplicate[:, None], noise[partner] + 0.03 * jitter, noise)
    values = centroid[clusters] + spread * noise
    return values.astype(jnp.bfloat16)


def setup_inputs(seed: int = 0) -> dict:
    key_list = jax.random.split(jax.random.key(seed), 3)
    return {
        "embeddings": draw_embeddings(jax.random.fold_in(key_list[2], 71), 0),
        "cluster_ids": draw_cluster_ids(jax.random.fold_in(key_list[2], 71), 0),
    }


def normalize_rows(embeddings):
    values = embeddings.astype(jnp.float32)
    scale = lax.rsqrt(lax.optimization_barrier(jnp.mean(values * values, axis=1, keepdims=True)) + 1e-06) / math.sqrt(values.shape[1])
    return (values * scale).astype(jnp.bfloat16)

def reference(embeddings, cluster_ids):
    unit = normalize_rows(embeddings)
    owner_of = (cluster_ids // CL_OWN).astype(jnp.int32)
    order = jnp.argsort(owner_of, stable=True).astype(jnp.int32)
    counts = lax.optimization_barrier(jnp.sum((owner_of[:, None] == jnp.arange(N_OWN, dtype=jnp.int32)[None, :]).astype(jnp.int32), axis=0))
    offsets = (jnp.cumsum(counts) - counts).astype(jnp.int32)
    window = N_SRC * N_OWN * CAP
    sorted_unit = jnp.concatenate([unit[order], jnp.zeros((window, unit.shape[1]), jnp.bfloat16)], axis=0)
    sorted_cluster = jnp.concatenate([cluster_ids[order].astype(jnp.int32), jnp.full((window,), -1, jnp.int32)])
    sorted_place = jnp.concatenate([order, jnp.full((window,), -1, jnp.int32)])

    def one_owner(best, owner):
        offset = offsets[owner]
        rows = lax.dynamic_slice_in_dim(sorted_unit, offset, window, 0)
        groups = lax.dynamic_slice_in_dim(sorted_cluster, offset, window, 0)
        places = lax.dynamic_slice_in_dim(sorted_place, offset, window, 0)
        scores = jnp.dot(rows, rows.T, preferred_element_type=jnp.float32)
        same_group = (groups[:, None] == groups[None, :]) & (places[:, None] != places[None, :])
        found = lax.optimization_barrier(jnp.max(jnp.where(same_group, scores, jnp.float32(-1.0)), axis=1))
        valid = jnp.arange(window, dtype=jnp.int32) < counts[owner]
        before = lax.dynamic_slice_in_dim(best, offset, window, 0)
        best = lax.dynamic_update_slice_in_dim(best, jnp.where(valid, found, before), offset, 0)
        return (best, 0)
    start = jnp.full((DOCS + window,), -1.0, jnp.float32)
    best, unused = lax.scan(one_owner, start, jnp.arange(N_OWN, dtype=jnp.int32))
    return jnp.zeros((DOCS,), jnp.float32).at[order].set(best[:DOCS])
```

```python
import functools
import math

import jax
import jax.numpy as jnp
from jax import lax
from jax.experimental import pallas as pl
from jax.experimental.pallas import tpu as pltpu
from jax.sharding import PartitionSpec as P

MESH = pl.DeviceIdType.MESH
F32, BF16, I32 = jnp.float32, jnp.bfloat16, jnp.int32

D = 1024
ROWS = 192
CAP = 12
OWNERS = 32
DEVS = 128
CL_OWN = 32
QUARTERS = 4
QW = D // QUARTERS
BLK = QUARTERS * CAP
GRP = 16
NGRP = DEVS // GRP
GROWS = GRP * CAP
RETW = 256


def home_of(owner):
    y, z, c = owner // 8, lax.rem(owner // 2, 4), lax.rem(owner, 2)
    return lax.rem(y + z + 2 * c, 4), owner


def shard_at(src, own):
    y, z, c = own // 8, lax.rem(own // 2, 4), lax.rem(own, 2)
    return lax.rem(y + z + 2 * c, 4) == src, own


def slot_of(src, own):
    y, z, c = own // 8, lax.rem(own // 2, 4), lax.rem(own, 2)
    return z * 32 + y * 8 + src * 2 + c


def device_at(slot):
    z, y, x, c = slot // 32, lax.rem(slot // 8, 4), lax.rem(slot // 2, 4), lax.rem(slot, 2)
    return x, y * 8 + z * 2 + c


def div12(v):
    return (v * 5462) >> 16


def dot_nn(a, b):
    return lax.dot_general(a, b, (((1,), (0,)), ((), ())), preferred_element_type=F32)


def dot_nt(a, b):
    return lax.dot_general(a, b, (((1,), (1,)), ((), ())), preferred_element_type=F32)


def dot_tn(a, b):
    return lax.dot_general(a, b, (((0,), (0,)), ((), ())), preferred_element_type=F32)


def iota(shape, dim):
    return lax.broadcasted_iota(I32, shape, dim)


def swap_matrix():
    i, j = iota((GROWS, GROWS), 0), iota((GROWS, GROWS), 1)
    ab = div12(i)
    a, b = ab >> 2, ab & 3
    return (j == b * BLK + a * CAP + (i - ab * CAP)).astype(BF16)


def kernel(
    emb_ref, ids_ref, out_ref,
    send, meta_send, recv, meta_recv, rows, id_col, id_row, best, back,
    send_sem, meta_send_sem, recv_sem, meta_recv_sem, back_send_sem, back_sem,
):
    src, own = lax.axis_index("src"), lax.axis_index("own")
    is_home, shard = shard_at(src, own)
    slot = slot_of(src, own)

    barrier = pltpu.get_barrier_semaphore()

    @pl.when(is_home)
    def _():
        def greet(i, carry):
            s, o = device_at(lax.rem(slot + i, DEVS))
            pl.semaphore_signal(barrier, inc=1, device_id=(s, o), device_id_type=MESH)
            return carry

        lax.fori_loop(1, DEVS, greet, 0)

    ids = ids_ref[...]
    owner = ids >> 5
    onehot = iota((OWNERS, ROWS), 0) == owner
    onehot_b = onehot.astype(BF16)
    upto = (iota((ROWS, ROWS), 0) <= iota((ROWS, ROWS), 1)).astype(BF16)
    counts = dot_nn(onehot_b, upto)
    rank = jnp.sum(jnp.where(onehot, counts, 0.0), axis=0, keepdims=True).astype(I32) - 1
    place = owner * CAP + rank
    pick = (iota((OWNERS * CAP, ROWS), 0) == place).astype(BF16)

    local = (ids - owner * CL_OWN + 1).astype(F32)
    by_rank = jnp.where(iota((128, ROWS), 0) == rank, local, 0.0).astype(BF16)
    meta_send[...] = (dot_nt(onehot_b, by_rank) - 1.0).reshape(OWNERS, 1, 128)

    values = emb_ref[...].astype(F32)
    mean = jnp.sum(values * values, axis=1, keepdims=True) * (1.0 / D)
    scale = lax.rsqrt(mean + 1e-06) * (1.0 / math.sqrt(D))
    unit = (values * scale).astype(BF16)
    packed = dot_nn(pick, unit).astype(BF16)
    swap = swap_matrix()
    for k in range(OWNERS // 4):
        part = packed[k * BLK : (k + 1) * BLK]
        stacked = jnp.concatenate([part[:, q * QW : (q + 1) * QW] for q in range(QUARTERS)], axis=0)
        send[pl.ds(4 * k, 4)] = dot_nn(swap, stacked).astype(BF16).reshape(4, BLK, QW)

    @pl.when(is_home)
    def _():
        pl.semaphore_wait(barrier, OWNERS - 1)

    @pl.when(jnp.logical_not(is_home))
    def _():
        pl.semaphore_wait(barrier, OWNERS)

    group = slot // GRP

    def give(i, carry):
        to = lax.rem(own + i, OWNERS)
        s, o = home_of(to)
        here = (s == src) & (o == own)

        @pl.when(jnp.logical_not(here))
        def _():
            pltpu.make_async_remote_copy(
                meta_send.at[to], meta_recv.at[slot], meta_send_sem, meta_recv_sem.at[group],
                device_id=(s, o), device_id_type=MESH,
            ).start()
            pltpu.make_async_remote_copy(
                send.at[to], recv.at[slot], send_sem, recv_sem.at[group],
                device_id=(s, o), device_id_type=MESH,
            ).start()

        @pl.when(here)
        def _():
            pltpu.make_async_copy(meta_send.at[to], meta_recv.at[slot], meta_recv_sem.at[group]).start()
            pltpu.make_async_copy(send.at[to], recv.at[slot], recv_sem.at[group]).start()

        return carry

    lax.fori_loop(0, OWNERS, give, 0)

    @pl.when(is_home)
    def _():
        lane_of = iota((GRP, GROWS), 1)
        spread = (div12(lane_of) == iota((GRP, GROWS), 0)).astype(BF16)
        nth_row = iota((GRP, GROWS), 0) == lane_of - div12(lane_of) * CAP
        sub = iota((GROWS, 128), 0)
        nth_col = iota((GROWS, 128), 1) == sub - div12(sub) * CAP
        not_self = iota((GROWS, GROWS), 0) != iota((GROWS, GROWS), 1)
        best[...] = jnp.full(best.shape, -1.0, F32)

        def one_group(g, carry):
            first = pl.multiple_of(g * GRP, GRP)
            block = meta_recv.at[pl.ds(first, GRP)]
            pltpu.make_async_copy(block, block, meta_recv_sem.at[g]).wait()
            block = recv.at[pl.ds(first, GRP)]
            pltpu.make_async_copy(block, block, recv_sem.at[g]).wait()
            ids_g = meta_recv[pl.ds(first, GRP)].reshape(GRP, 128).astype(BF16)
            wide = dot_tn(spread, ids_g)
            col_g = jnp.sum(jnp.where(nth_col, wide, 0.0), axis=1, keepdims=True)
            wide = dot_tn(ids_g, spread)[:GRP]
            row_g = jnp.sum(jnp.where(nth_row, wide, 0.0), axis=0, keepdims=True)
            id_col[g] = col_g
            id_row[g] = row_g
            for k in range(GRP // 4):
                four = recv[pl.ds(first + 4 * k, 4)].reshape(GROWS, QW)
                turned = dot_nn(swap, four).astype(BF16)
                at = pl.ds(pl.multiple_of(g * GROWS + k * BLK, 16), BLK)
                for q in range(QUARTERS):
                    rows[at, q * QW : (q + 1) * QW] = turned[q * BLK : (q + 1) * BLK]
            mine = rows[pl.ds(pl.multiple_of(g * GROWS, 16), GROWS), :]
            scores = dot_nt(mine, mine)
            keep = (col_g == row_g) & not_self
            found = jnp.max(jnp.where(keep, scores, -1.0), axis=0, keepdims=True)

            def earlier(h, found):
                other = rows[pl.ds(pl.multiple_of(h * GROWS, 16), GROWS), :]
                scores = dot_nt(other, mine)
                top = jnp.max(jnp.where(id_col[h] == row_g, scores, -1.0), axis=0, keepdims=True)
                scores = dot_nt(mine, other)
                top_h = jnp.max(jnp.where(col_g == id_row[h], scores, -1.0), axis=0, keepdims=True)
                best[h, :, :GROWS] = jnp.maximum(best[h, :, :GROWS], top_h)
                return jnp.maximum(found, top)

            found = lax.fori_loop(0, g, earlier, found)
            best[g, :, :GROWS] = jnp.maximum(found, -1.0)
            return carry

        lax.fori_loop(0, NGRP, one_group, 0)

        def give_back(i, carry):
            to = lax.rem(slot + i, DEVS)
            pltpu.make_async_remote_copy(
                best.at[to // GRP], back.at[shard], back_send_sem, back_sem,
                device_id=device_at(to), device_id_type=MESH,
            ).start()
            return carry

        lax.fori_loop(1, DEVS, give_back, 0)
        pltpu.make_async_copy(best.at[group], back.at[shard], back_sem).start()

    pltpu.make_async_copy(back, back, back_sem).wait()
    got = back[...].reshape(OWNERS, RETW)
    high = got.astype(BF16)
    rest = got - high.astype(F32)
    mid = rest.astype(BF16)
    low = (rest - mid.astype(F32)).astype(BF16)
    wide = dot_tn(high, onehot_b) + dot_tn(mid, onehot_b) + dot_tn(low, onehot_b)
    lane = lax.rem(slot, GRP) * CAP + rank
    out_ref[...] = jnp.sum(jnp.where(iota((RETW, ROWS), 0) == lane, wide, 0.0), axis=0, keepdims=True)

    @pl.when(is_home)
    def _():
        pltpu.make_async_copy(send.at[pl.ds(0, OWNERS - 1)], send.at[pl.ds(0, OWNERS - 1)], send_sem).wait()
        part = meta_send.at[pl.ds(0, OWNERS - 1)]
        pltpu.make_async_copy(part, part, meta_send_sem).wait()

        def sent(i, carry):
            pltpu.make_async_copy(best.at[0], best.at[0], back_send_sem).wait()
            return carry

        lax.fori_loop(1, DEVS, sent, 0)

    @pl.when(jnp.logical_not(is_home))
    def _():
        pltpu.make_async_copy(send, send, send_sem).wait()
        pltpu.make_async_copy(meta_send, meta_send, meta_send_sem).wait()


def shards(embeddings, cluster_ids):
    dma = pltpu.SemaphoreType.DMA
    out = pl.pallas_call(
        kernel,
        out_shape=jax.ShapeDtypeStruct((1, ROWS), F32),
        in_specs=[pl.BlockSpec(memory_space=pltpu.VMEM)] * 2,
        out_specs=pl.BlockSpec(memory_space=pltpu.VMEM),
        scratch_shapes=[
            pltpu.VMEM((OWNERS, BLK, QW), BF16),
            pltpu.VMEM((OWNERS, 1, 128), F32),
            pltpu.VMEM((DEVS, BLK, QW), BF16),
            pltpu.VMEM((DEVS, 1, 128), F32),
            pltpu.VMEM((DEVS * CAP, D), BF16),
            pltpu.VMEM((NGRP, GROWS, 1), F32),
            pltpu.VMEM((NGRP, 1, GROWS), F32),
            pltpu.VMEM((NGRP, 1, RETW), F32),
            pltpu.VMEM((OWNERS, 1, RETW), F32),
            dma, dma, dma((NGRP,)), dma((NGRP,)), dma, dma,
        ],
        compiler_params=pltpu.CompilerParams(
            collective_id=0, has_side_effects=True, vmem_limit_bytes=40 << 20
        ),
    )(embeddings, cluster_ids.reshape(1, ROWS))
    return out.reshape(ROWS)


def solution(mesh):
    in_specs = (P(("src", "own"), None), P(("src", "own")))
    out_specs = P(("src", "own"))
    return jax.shard_map(shards, mesh=mesh, in_specs=in_specs, out_specs=out_specs, check_vma=False)
```

```python
import functools
import math

import jax
import jax.numpy as jnp
from jax import lax
from jax.experimental import pallas as pl
from jax.experimental.pallas import tpu as pltpu
from jax.sharding import PartitionSpec as P

MESH = pl.DeviceIdType.MESH
F32, BF16, I32 = jnp.float32, jnp.bfloat16, jnp.int32

D = 1024
ROWS = 192
CAP = 12
OWNERS = 32
SLOTS = 64
CL_OWN = 32
QUARTERS = 4
QW = D // QUARTERS
BLK = QUARTERS * CAP
GRP = 16
NGRP = SLOTS // GRP
GROWS = GRP * CAP
HROWS = SLOTS * CAP
NT = 256
RETW = 256


def home_of(owner):
    y, z = owner // 8, lax.rem(owner // 2, 4)
    return lax.rem(y + z + 2 * lax.rem(owner, 2), 4), owner // 2


def shard_at(src, line):
    turn = lax.rem(src - line // 4 - lax.rem(line, 4) + 8, 4)
    return lax.rem(turn, 2) == 0, line * 2 + turn // 2


def div12(v):
    return (v * 5462) >> 16


def dot_nn(a, b):
    return lax.dot_general(a, b, (((1,), (0,)), ((), ())), preferred_element_type=F32)


def dot_nt(a, b):
    return lax.dot_general(a, b, (((1,), (1,)), ((), ())), preferred_element_type=F32)


def dot_tn(a, b):
    return lax.dot_general(a, b, (((0,), (0,)), ((), ())), preferred_element_type=F32)


def iota(shape, dim):
    return lax.broadcasted_iota(I32, shape, dim)


def swap_matrix():
    i, j = iota((GROWS, GROWS), 0), iota((GROWS, GROWS), 1)
    ab = div12(i)
    a, b = ab >> 2, ab & 3
    return (j == b * BLK + a * CAP + (i - ab * CAP)).astype(BF16)


def kernel(
    emb_hbm, ids_ref, out_ref,
    emb_ref, send, meta_send, recv, meta_recv, rows, theirs, meta_theirs, id_col, best, back,
    emb_sem, send_sem, meta_send_sem, recv_sem, meta_recv_sem, pass_sem, theirs_sem,
    meta_pass_sem, meta_theirs_sem, back_send_sem, back_sem,
):
    src, own = lax.axis_index("src"), lax.axis_index("own")
    line, core = own // 2, lax.rem(own, 2)
    is_home, shard = shard_at(src, line)
    slot = line * 4 + src
    partner = (src, own + 1 - 2 * core)

    barrier = pltpu.get_barrier_semaphore()
    fetch = pltpu.make_async_copy(emb_hbm, emb_ref, emb_sem)
    fetch.start()

    @pl.when(is_home)
    def _():
        pl.semaphore_signal(barrier, inc=1, device_id=partner, device_id_type=MESH)

        def greet(i, carry):
            to = lax.rem(slot + i, SLOTS)
            device = (lax.rem(to, 4), (to // 4) * 2 + core)
            pl.semaphore_signal(barrier, inc=1, device_id=device, device_id_type=MESH)
            return carry

        lax.fori_loop(1, SLOTS, greet, 0)

    ids = ids_ref[...]
    owner = ids >> 5
    onehot = iota((OWNERS, ROWS), 0) == owner
    onehot_b = onehot.astype(BF16)
    upto = (iota((ROWS, ROWS), 0) <= iota((ROWS, ROWS), 1)).astype(BF16)
    counts = dot_nn(onehot_b, upto)
    rank = jnp.sum(jnp.where(onehot, counts, 0.0), axis=0, keepdims=True).astype(I32) - 1
    place = owner * CAP + rank
    pick = (iota((OWNERS * CAP, ROWS), 0) == place).astype(BF16)

    local = (ids - owner * CL_OWN + 1).astype(F32)
    by_rank = jnp.where(iota((128, ROWS), 0) == rank, local, 0.0).astype(BF16)
    meta_send[...] = (dot_nt(onehot_b, by_rank) - 1.0).reshape(OWNERS, 1, 128)

    fetch.wait()
    values = emb_ref[...].astype(F32)
    mean = jnp.sum(values * values, axis=1, keepdims=True) * (1.0 / D)
    scale = lax.rsqrt(mean + 1e-06) * (1.0 / math.sqrt(D))
    unit = (values * scale).astype(BF16)
    packed = dot_nn(pick, unit).astype(BF16)
    swap = swap_matrix()
    for k in range(OWNERS // 4):
        part = packed[k * BLK : (k + 1) * BLK]
        stacked = jnp.concatenate([part[:, q * QW : (q + 1) * QW] for q in range(QUARTERS)], axis=0)
        send[pl.ds(4 * k, 4)] = dot_nn(swap, stacked).astype(BF16).reshape(4, BLK, QW)

    pl.semaphore_wait(barrier, OWNERS)

    def give_meta(i, carry):
        to = lax.rem(own + i, OWNERS)
        s, at = home_of(to)
        here = (s == src) & (at == line)

        @pl.when(jnp.logical_not(here))
        def _():
            pltpu.make_async_remote_copy(
                meta_send.at[to], meta_recv.at[slot], meta_send_sem, meta_recv_sem,
                device_id=(s, at * 2 + core), device_id_type=MESH,
            ).start()

        @pl.when(here)
        def _():
            pltpu.make_async_copy(meta_send.at[to], meta_recv.at[slot], meta_recv_sem).start()

        return carry

    lax.fori_loop(0, OWNERS, give_meta, 0)
    group = slot // GRP

    def give(i, carry):
        to = lax.rem(own + i, OWNERS)
        s, at = home_of(to)
        here = (s == src) & (at == line)

        @pl.when(jnp.logical_not(here))
        def _():
            pltpu.make_async_remote_copy(
                send.at[to], recv.at[slot], send_sem, recv_sem.at[group],
                device_id=(s, at * 2 + core), device_id_type=MESH,
            ).start()

        @pl.when(here)
        def _():
            pltpu.make_async_copy(send.at[to], recv.at[slot], recv_sem.at[group]).start()

        return carry

    lax.fori_loop(0, OWNERS, give, 0)

    @pl.when(is_home)
    def _():
        lane_of = iota((GRP, GROWS), 1)
        spread = (div12(lane_of) == iota((GRP, GROWS), 0)).astype(BF16)
        nth_row = iota((GRP, GROWS), 0) == lane_of - div12(lane_of) * CAP
        sub = iota((GROWS, 128), 0)
        nth_col = iota((GROWS, 128), 1) == sub - div12(sub) * CAP

        pltpu.make_async_copy(meta_recv, meta_recv, meta_recv_sem).wait()
        meta_pass = pltpu.make_async_remote_copy(
            meta_recv, meta_theirs, meta_pass_sem, meta_theirs_sem,
            device_id=partner, device_id_type=MESH,
        )
        meta_pass.start()

        def down(ref, g):
            ids_g = ref[pl.ds(g * GRP, GRP)].reshape(GRP, 128).astype(BF16)
            wide = dot_tn(spread, ids_g)
            return ids_g, jnp.sum(jnp.where(nth_col, wide, 0.0), axis=1, keepdims=True)

        along = []
        for g in range(NGRP):
            ids_g, col_g = down(meta_recv, g)
            id_col[0, g * GROWS : (g + 1) * GROWS] = col_g
            wide = dot_tn(ids_g, spread)[:GRP]
            along.append(jnp.sum(jnp.where(nth_row, wide, 0.0), axis=0, keepdims=True))
        along = jnp.concatenate(along, axis=1)
        meta_pass.wait_recv()
        for g in range(NGRP):
            id_col[1, g * GROWS : (g + 1) * GROWS] = down(meta_theirs, g)[1]

        def passing(g):
            part = pl.ds(g * GROWS, GROWS)
            return pltpu.make_async_remote_copy(
                rows.at[part], theirs.at[part], pass_sem, theirs_sem,
                device_id=partner, device_id_type=MESH,
            )

        for g in range(NGRP):
            block = recv.at[pl.ds(g * GRP, GRP)]
            pltpu.make_async_copy(block, block, recv_sem.at[g]).wait()
            for k in range(GRP // 4):
                four = recv[pl.ds(g * GRP + 4 * k, 4)].reshape(GROWS, QW)
                turned = dot_nn(swap, four).astype(BF16)
                at = g * GROWS + k * BLK
                for q in range(QUARTERS):
                    rows[at : at + BLK, q * QW : (q + 1) * QW] = turned[q * BLK : (q + 1) * BLK]
            passing(g).start()

        found = []
        for n in range(HROWS // NT):
            mine = rows[n * NT : (n + 1) * NT, :]
            scores = dot_nt(rows[...], mine)
            keep = (id_col[0] == along[:, n * NT : (n + 1) * NT]) & (
                iota((HROWS, NT), 0) != iota((HROWS, NT), 1) + n * NT
            )
            found.append(jnp.max(jnp.where(keep, scores, -1.0), axis=0, keepdims=True))
        pltpu.make_async_copy(theirs, theirs, theirs_sem).wait()
        for n in range(HROWS // NT):
            mine = rows[n * NT : (n + 1) * NT, :]
            scores = dot_nt(theirs[...], mine)
            keep = id_col[1] == along[:, n * NT : (n + 1) * NT]
            top = jnp.max(jnp.where(keep, scores, -1.0), axis=0, keepdims=True)
            found[n] = jnp.maximum(jnp.maximum(found[n], top), -1.0)
        found = jnp.concatenate(found, axis=1)
        for g in range(NGRP):
            best[g, :, :GROWS] = found[:, g * GROWS : (g + 1) * GROWS]

        def give_back(to, carry):
            @pl.when(to != slot)
            def _():
                pltpu.make_async_remote_copy(
                    best.at[to // GRP], back.at[shard], back_send_sem, back_sem,
                    device_id=(lax.rem(to, 4), (to // 4) * 2 + core), device_id_type=MESH,
                ).start()

            @pl.when(to == slot)
            def _():
                pltpu.make_async_copy(best.at[group], back.at[shard], back_sem).start()

            return carry

        lax.fori_loop(0, SLOTS, give_back, 0)

    pltpu.make_async_copy(back, back, back_sem).wait()
    got = back[...].reshape(OWNERS, RETW)
    high = got.astype(BF16)
    rest = got - high.astype(F32)
    mid = rest.astype(BF16)
    low = (rest - mid.astype(F32)).astype(BF16)
    wide = dot_tn(high, onehot_b) + dot_tn(mid, onehot_b) + dot_tn(low, onehot_b)
    lane = lax.rem(slot, GRP) * CAP + rank
    out_ref[...] = jnp.sum(jnp.where(iota((RETW, ROWS), 0) == lane, wide, 0.0), axis=0, keepdims=True)

    @pl.when(is_home)
    def _():
        part = send.at[pl.ds(0, OWNERS - 1)]
        pltpu.make_async_copy(part, part, send_sem).wait()
        part = meta_send.at[pl.ds(0, OWNERS - 1)]
        pltpu.make_async_copy(part, part, meta_send_sem).wait()
        pltpu.make_async_copy(meta_recv, meta_recv, meta_pass_sem).wait()
        pltpu.make_async_copy(rows, rows, pass_sem).wait()
        pltpu.make_async_copy(back, back, back_send_sem).wait()
        part = back.at[pl.ds(0, OWNERS - 1)]
        pltpu.make_async_copy(part, part, back_send_sem).wait()

    @pl.when(jnp.logical_not(is_home))
    def _():
        pltpu.make_async_copy(send, send, send_sem).wait()
        pltpu.make_async_copy(meta_send, meta_send, meta_send_sem).wait()


def shards(embeddings, cluster_ids):
    dma = pltpu.SemaphoreType.DMA
    out = pl.pallas_call(
        kernel,
        out_shape=jax.ShapeDtypeStruct((1, ROWS), F32),
        in_specs=[pl.BlockSpec(memory_space=pl.ANY), pl.BlockSpec(memory_space=pltpu.VMEM)],
        out_specs=pl.BlockSpec(memory_space=pltpu.VMEM),
        scratch_shapes=[
            pltpu.VMEM((ROWS, D), BF16),
            pltpu.VMEM((OWNERS, BLK, QW), BF16),
            pltpu.VMEM((OWNERS, 1, 128), F32),
            pltpu.VMEM((SLOTS, BLK, QW), BF16),
            pltpu.VMEM((SLOTS, 1, 128), F32),
            pltpu.VMEM((HROWS, D), BF16),
            pltpu.VMEM((HROWS, D), BF16),
            pltpu.VMEM((SLOTS, 1, 128), F32),
            pltpu.VMEM((2, HROWS, 1), F32),
            pltpu.VMEM((NGRP, 1, RETW), F32),
            pltpu.VMEM((OWNERS, 1, RETW), F32),
            dma, dma, dma, dma((NGRP,)), dma, dma, dma, dma, dma, dma, dma,
        ],
        compiler_params=pltpu.CompilerParams(
            collective_id=0, has_side_effects=True, vmem_limit_bytes=40 << 20
        ),
    )(embeddings, cluster_ids.reshape(1, ROWS))
    return out.reshape(ROWS)


def solution(mesh):
    in_specs = (P(("src", "own"), None), P(("src", "own")))
    out_specs = P(("src", "own"))
    return jax.shard_map(shards, mesh=mesh, in_specs=in_specs, out_specs=out_specs, check_vma=False)
```

```python
import functools
import math

import jax
import jax.numpy as jnp
from jax import lax
from jax.experimental import pallas as pl
from jax.experimental.pallas import tpu as pltpu
from jax.sharding import PartitionSpec as P

MESH = pl.DeviceIdType.MESH
F32, BF16, I32 = jnp.float32, jnp.bfloat16, jnp.int32

D = 1024
ROWS = 192
CAP = 12
OWNERS = 32
SLOTS = 64
CL_OWN = 32
QUARTERS = 4
QW = D // QUARTERS
BLK = QUARTERS * CAP
GRP = 16
NGRP = SLOTS // GRP
GROWS = GRP * CAP
HROWS = SLOTS * CAP
NT = 256
RETW = 256


def home_of(owner):
    return lax.rem(owner, 4), lax.rem(owner // 4, 4), (owner // 16) * 2


def gray(v):
    return v + v // 2 - 2 * (v // 3)


def at(x, y, z, core):
    return x, y * 8 + z * 2 + core


def div12(v):
    return (v * 5462) >> 16


def dot_nn(a, b):
    return lax.dot_general(a, b, (((1,), (0,)), ((), ())), preferred_element_type=F32)


def dot_nt(a, b):
    return lax.dot_general(a, b, (((1,), (1,)), ((), ())), preferred_element_type=F32)


def dot_tn(a, b):
    return lax.dot_general(a, b, (((0,), (0,)), ((), ())), preferred_element_type=F32)


def iota(shape, dim):
    return lax.broadcasted_iota(I32, shape, dim)


def swap_matrix():
    i, j = iota((GROWS, GROWS), 0), iota((GROWS, GROWS), 1)
    ab = div12(i)
    a, b = ab >> 2, ab & 3
    return (j == b * BLK + a * CAP + (i - ab * CAP)).astype(BF16)


def kernel(
    emb_hbm, ids_ref, out_ref,
    emb_ref, send, meta_send, recv, meta_recv, rows, theirs, meta_theirs, id_col, best, back,
    emb_sem, send_sem, meta_send_sem, recv_sem, meta_recv_sem, pass_sem, theirs_sem,
    meta_pass_sem, meta_theirs_sem, back_send_sem, back_sem,
):
    src, own = lax.axis_index("src"), lax.axis_index("own")
    y, z, core = own // 8, lax.rem(own // 2, 4), lax.rem(own, 2)
    is_home, shard = lax.rem(z, 2) == 0, (z // 2) * 16 + y * 4 + src
    is_relay = (lax.rem(z, 2) == 1) & (core == 1)
    seat = y * 4 + src
    partner = (src, own + 1 - 2 * core)

    barrier = pltpu.get_barrier_semaphore()
    fetch = pltpu.make_async_copy(emb_hbm, emb_ref, emb_sem)
    fetch.start()

    @pl.when(is_home)
    def _():
        pl.semaphore_signal(barrier, inc=1, device_id=partner, device_id_type=MESH)

        def greet(i, carry):
            to = lax.rem(z * 16 + seat + i, SLOTS)
            device = at(lax.rem(to, 4), lax.rem(to // 4, 4), to // 16, core)
            pl.semaphore_signal(barrier, inc=1, device_id=device, device_id_type=MESH)
            return carry

        lax.fori_loop(1, SLOTS, greet, 0)

    @pl.when(is_relay)
    def _():
        def greet(i, carry):
            device = at(lax.rem(i, 4), i // 4, lax.rem(z + 1, 4), core)
            pl.semaphore_signal(barrier, inc=1, device_id=device, device_id_type=MESH)
            return carry

        lax.fori_loop(0, GRP, greet, 0)

    ids = ids_ref[...]
    owner = ids >> 5
    onehot = iota((OWNERS, ROWS), 0) == owner
    onehot_b = onehot.astype(BF16)
    upto = (iota((ROWS, ROWS), 0) <= iota((ROWS, ROWS), 1)).astype(BF16)
    counts = dot_nn(onehot_b, upto)
    rank = jnp.sum(jnp.where(onehot, counts, 0.0), axis=0, keepdims=True).astype(I32) - 1
    place = owner * CAP + rank
    pick = (iota((OWNERS * CAP, ROWS), 0) == place).astype(BF16)

    local = (ids - owner * CL_OWN + 1).astype(F32)
    by_rank = jnp.where(iota((128, ROWS), 0) == rank, local, 0.0).astype(BF16)
    meta_send[...] = (dot_nt(onehot_b, by_rank) - 1.0).reshape(OWNERS, 1, 128)

    fetch.wait()
    values = emb_ref[...].astype(F32)
    mean = jnp.sum(values * values, axis=1, keepdims=True) * (1.0 / D)
    scale = lax.rsqrt(mean + 1e-06) * (1.0 / math.sqrt(D))
    unit = (values * scale).astype(BF16)
    packed = dot_nn(pick, unit).astype(BF16)
    swap = swap_matrix()
    for k in range(OWNERS // 4):
        part = packed[k * BLK : (k + 1) * BLK]
        stacked = jnp.concatenate([part[:, q * QW : (q + 1) * QW] for q in range(QUARTERS)], axis=0)
        send[pl.ds(4 * k, 4)] = dot_nn(swap, stacked).astype(BF16).reshape(4, BLK, QW)

    @pl.when(is_home & (core == 1))
    def _():
        pl.semaphore_wait(barrier, OWNERS + GRP)

    @pl.when(jnp.logical_not(is_home & (core == 1)))
    def _():
        pl.semaphore_wait(barrier, OWNERS)

    plane = lax.rem(z // 2 + core, 2)

    def target(i):
        to = lax.rem(plane + i // 16, 2) * 16 + lax.rem(seat + i, 16)
        hx, hy, hz = home_of(to)
        away = lax.rem(z - hz + 4, 4)
        here = (hx == src) & (hy == y) & (away == 0)
        return to, hx, hy, hz, away, here, gray(away)

    def give_meta(i, carry):
        to, hx, hy, hz, away, here, group = target(i)
        slot = group * GRP + seat

        @pl.when(jnp.logical_not(here))
        def _():
            pltpu.make_async_remote_copy(
                meta_send.at[to], meta_recv.at[slot], meta_send_sem, meta_recv_sem,
                device_id=at(hx, hy, hz, core), device_id_type=MESH,
            ).start()

        @pl.when(here)
        def _():
            pltpu.make_async_copy(meta_send.at[to], meta_recv.at[slot], meta_recv_sem).start()

        return carry

    lax.fori_loop(0, OWNERS, give_meta, 0)

    def give(i, carry):
        to, hx, hy, hz, away, here, group = target(i)
        slot = group * GRP + seat
        via = (away == 2) & (core == 1)

        @pl.when(via)
        def _():
            pltpu.make_async_remote_copy(
                send.at[to], recv.at[seat], send_sem, recv_sem.at[y],
                device_id=at(hx, hy, hz + 1, core), device_id_type=MESH,
            ).start()

        @pl.when(jnp.logical_not(here | via))
        def _():
            pltpu.make_async_remote_copy(
                send.at[to], recv.at[slot], send_sem, recv_sem.at[group],
                device_id=at(hx, hy, hz, core), device_id_type=MESH,
            ).start()

        @pl.when(here)
        def _():
            pltpu.make_async_copy(send.at[to], recv.at[slot], recv_sem.at[group]).start()

        return carry

    lax.fori_loop(0, OWNERS, give, 0)

    def onward(k):
        return pltpu.make_async_remote_copy(
            recv.at[pl.ds(4 * k, 4)], recv.at[pl.ds(3 * GRP + 4 * k, 4)], pass_sem, recv_sem.at[3],
            device_id=at(src, y, z - 1, core), device_id_type=MESH,
        )

    @pl.when(is_relay)
    def _():
        for k in range(4):
            block = recv.at[pl.ds(4 * k, 4)]
            pltpu.make_async_copy(block, block, recv_sem.at[k]).wait()
            onward(k).start()

    @pl.when(is_home)
    def _():
        lane_of = iota((GRP, GROWS), 1)
        spread = (div12(lane_of) == iota((GRP, GROWS), 0)).astype(BF16)
        nth_row = iota((GRP, GROWS), 0) == lane_of - div12(lane_of) * CAP
        sub = iota((GROWS, 128), 0)
        nth_col = iota((GROWS, 128), 1) == sub - div12(sub) * CAP

        pltpu.make_async_copy(meta_recv, meta_recv, meta_recv_sem).wait()
        meta_pass = pltpu.make_async_remote_copy(
            meta_recv, meta_theirs, meta_pass_sem, meta_theirs_sem,
            device_id=partner, device_id_type=MESH,
        )
        meta_pass.start()

        def down(ref, g):
            ids_g = ref[pl.ds(g * GRP, GRP)].reshape(GRP, 128).astype(BF16)
            wide = dot_tn(spread, ids_g)
            return ids_g, jnp.sum(jnp.where(nth_col, wide, 0.0), axis=1, keepdims=True)

        along = []
        for g in range(NGRP):
            ids_g, col_g = down(meta_recv, g)
            id_col[0, g * GROWS : (g + 1) * GROWS] = col_g
            wide = dot_tn(ids_g, spread)[:GRP]
            along.append(jnp.sum(jnp.where(nth_row, wide, 0.0), axis=0, keepdims=True))
        along = jnp.concatenate(along, axis=1)
        meta_pass.wait_recv()
        for g in range(NGRP):
            id_col[1, g * GROWS : (g + 1) * GROWS] = down(meta_theirs, g)[1]

        def passing(g):
            part = pl.ds(g * GROWS, GROWS)
            return pltpu.make_async_remote_copy(
                rows.at[part], theirs.at[part], pass_sem, theirs_sem,
                device_id=partner, device_id_type=MESH,
            )

        for g in range(NGRP):
            block = recv.at[pl.ds(g * GRP, GRP)]
            pltpu.make_async_copy(block, block, recv_sem.at[g]).wait()
            for k in range(GRP // 4):
                four = recv[pl.ds(g * GRP + 4 * k, 4)].reshape(GROWS, QW)
                turned = dot_nn(swap, four).astype(BF16)
                first = g * GROWS + k * BLK
                for q in range(QUARTERS):
                    rows[first : first + BLK, q * QW : (q + 1) * QW] = turned[q * BLK : (q + 1) * BLK]
            passing(g).start()

        found = []
        for n in range(HROWS // NT):
            mine = rows[n * NT : (n + 1) * NT, :]
            scores = dot_nt(rows[...], mine)
            keep = (id_col[0] == along[:, n * NT : (n + 1) * NT]) & (
                iota((HROWS, NT), 0) != iota((HROWS, NT), 1) + n * NT
            )
            found.append(jnp.max(jnp.where(keep, scores, -1.0), axis=0, keepdims=True))
        pltpu.make_async_copy(theirs, theirs, theirs_sem).wait()
        for n in range(HROWS // NT):
            mine = rows[n * NT : (n + 1) * NT, :]
            scores = dot_nt(theirs[...], mine)
            keep = id_col[1] == along[:, n * NT : (n + 1) * NT]
            top = jnp.max(jnp.where(keep, scores, -1.0), axis=0, keepdims=True)
            found[n] = jnp.maximum(jnp.maximum(found[n], top), -1.0)
        found = jnp.concatenate(found, axis=1)
        for g in range(NGRP):
            best[g, :, :GROWS] = found[:, g * GROWS : (g + 1) * GROWS]

        def give_back(to, carry):
            @pl.when(to != seat)
            def _():
                device = at(lax.rem(to, 4), lax.rem(to // 4, 4), lax.rem(z + gray(to // GRP), 4), core)
                pltpu.make_async_remote_copy(
                    best.at[to // GRP], back.at[shard], back_send_sem, back_sem,
                    device_id=device, device_id_type=MESH,
                ).start()

            @pl.when(to == seat)
            def _():
                pltpu.make_async_copy(best.at[0], back.at[shard], back_sem).start()

            return carry

        lax.fori_loop(0, SLOTS, give_back, 0)

    pltpu.make_async_copy(back, back, back_sem).wait()
    got = back[...].reshape(OWNERS, RETW)
    high = got.astype(BF16)
    rest = got - high.astype(F32)
    mid = rest.astype(BF16)
    low = (rest - mid.astype(F32)).astype(BF16)
    wide = dot_tn(high, onehot_b) + dot_tn(mid, onehot_b) + dot_tn(low, onehot_b)
    lane = seat * CAP + rank
    out_ref[...] = jnp.sum(jnp.where(iota((RETW, ROWS), 0) == lane, wide, 0.0), axis=0, keepdims=True)

    @pl.when(is_home)
    def _():
        part = send.at[pl.ds(0, OWNERS - 1)]
        pltpu.make_async_copy(part, part, send_sem).wait()
        part = meta_send.at[pl.ds(0, OWNERS - 1)]
        pltpu.make_async_copy(part, part, meta_send_sem).wait()
        pltpu.make_async_copy(meta_recv, meta_recv, meta_pass_sem).wait()
        pltpu.make_async_copy(rows, rows, pass_sem).wait()
        pltpu.make_async_copy(back, back, back_send_sem).wait()
        part = back.at[pl.ds(0, OWNERS - 1)]
        pltpu.make_async_copy(part, part, back_send_sem).wait()

    @pl.when(jnp.logical_not(is_home))
    def _():
        pltpu.make_async_copy(send, send, send_sem).wait()
        pltpu.make_async_copy(meta_send, meta_send, meta_send_sem).wait()

    @pl.when(is_relay)
    def _():
        part = recv.at[pl.ds(0, GRP)]
        pltpu.make_async_copy(part, part, pass_sem).wait()


def shards(embeddings, cluster_ids):
    dma = pltpu.SemaphoreType.DMA
    out = pl.pallas_call(
        kernel,
        out_shape=jax.ShapeDtypeStruct((1, ROWS), F32),
        in_specs=[pl.BlockSpec(memory_space=pl.ANY), pl.BlockSpec(memory_space=pltpu.VMEM)],
        out_specs=pl.BlockSpec(memory_space=pltpu.VMEM),
        scratch_shapes=[
            pltpu.VMEM((ROWS, D), BF16),
            pltpu.VMEM((OWNERS, BLK, QW), BF16),
            pltpu.VMEM((OWNERS, 1, 128), F32),
            pltpu.VMEM((SLOTS, BLK, QW), BF16),
            pltpu.VMEM((SLOTS, 1, 128), F32),
            pltpu.VMEM((HROWS, D), BF16),
            pltpu.VMEM((HROWS, D), BF16),
            pltpu.VMEM((SLOTS, 1, 128), F32),
            pltpu.VMEM((2, HROWS, 1), F32),
            pltpu.VMEM((NGRP, 1, RETW), F32),
            pltpu.VMEM((OWNERS, 1, RETW), F32),
            dma, dma, dma, dma((NGRP,)), dma, dma, dma, dma, dma, dma, dma,
        ],
        compiler_params=pltpu.CompilerParams(
            collective_id=0, has_side_effects=True, vmem_limit_bytes=40 << 20
        ),
    )(embeddings, cluster_ids.reshape(1, ROWS))
    return out.reshape(ROWS)


def solution(mesh):
    in_specs = (P(("src", "own"), None), P(("src", "own")))
    out_specs = P(("src", "own"))
    return jax.shard_map(shards, mesh=mesh, in_specs=in_specs, out_specs=out_specs, check_vma=False)
```

```python
import functools
import math

import jax
import jax.numpy as jnp
from jax import lax
from jax.experimental import pallas as pl
from jax.experimental.pallas import tpu as pltpu
from jax.sharding import PartitionSpec as P

MESH = pl.DeviceIdType.MESH
F32, BF16, I32 = jnp.float32, jnp.bfloat16, jnp.int32

D = 1024
ROWS = 192
CAP = 12
OWNERS = 32
SLOTS = 64
CL_OWN = 32
QUARTERS = 4
QW = D // QUARTERS
BLK = QUARTERS * CAP
GRP = 16
NGRP = SLOTS // GRP
GROWS = GRP * CAP
HROWS = SLOTS * CAP
HALF = HROWS // 2
RETW = 256


def home_of(owner):
    return lax.rem(owner, 4), lax.rem(owner // 4, 4), (owner // 16) * 2


def gray(v):
    return v + v // 2 - 2 * (v // 3)


def at(x, y, z, core):
    return x, y * 8 + z * 2 + core


def div12(v):
    return (v * 5462) >> 16


def dot_nn(a, b):
    return lax.dot_general(a, b, (((1,), (0,)), ((), ())), preferred_element_type=F32)


def dot_nt(a, b):
    return lax.dot_general(a, b, (((1,), (1,)), ((), ())), preferred_element_type=F32)


def dot_tn(a, b):
    return lax.dot_general(a, b, (((0,), (0,)), ((), ())), preferred_element_type=F32)


def iota(shape, dim):
    return lax.broadcasted_iota(I32, shape, dim)


def swap_matrix():
    i, j = iota((GROWS, GROWS), 0), iota((GROWS, GROWS), 1)
    ab = div12(i)
    a, b = ab >> 2, ab & 3
    return (j == b * BLK + a * CAP + (i - ab * CAP)).astype(BF16)


def kernel(
    emb_hbm, ids_hbm, out_ref,
    emb_ref, ids_ref, send, meta_send, recv, meta_recv, rows, theirs, meta_theirs, id_col, best, back,
    emb_sem, ids_sem, send_sem, meta_send_sem, recv_sem, meta_recv_sem, pass_sem, theirs_sem,
    meta_pass_sem, meta_theirs_sem, back_send_sem, back_sem,
):
    src, own = lax.axis_index("src"), lax.axis_index("own")
    y, z, core = own // 8, lax.rem(own // 2, 4), lax.rem(own, 2)
    is_home, shard = lax.rem(z, 2) == 0, (z // 2) * 16 + y * 4 + src
    is_relay = (lax.rem(z, 2) == 1) & (core == 1)
    seat = y * 4 + src
    partner = (src, own + 1 - 2 * core)

    barrier = pltpu.get_barrier_semaphore()
    fetch = pltpu.make_async_copy(emb_hbm, emb_ref, emb_sem)
    fetch_ids = pltpu.make_async_copy(ids_hbm, ids_ref, ids_sem)
    fetch_ids.start()
    fetch.start()

    @pl.when(is_home)
    def _():
        pl.semaphore_signal(barrier, inc=1, device_id=partner, device_id_type=MESH)

        def greet(i, carry):
            to = lax.rem(z * 16 + seat + i, SLOTS)
            device = at(lax.rem(to, 4), lax.rem(to // 4, 4), to // 16, core)
            pl.semaphore_signal(barrier, inc=1, device_id=device, device_id_type=MESH)
            return carry

        lax.fori_loop(1, SLOTS, greet, 0)

    @pl.when(is_relay)
    def _():
        def greet(i, carry):
            device = at(lax.rem(i, 4), i // 4, lax.rem(z + 1, 4), core)
            pl.semaphore_signal(barrier, inc=1, device_id=device, device_id_type=MESH)
            return carry

        lax.fori_loop(0, GRP, greet, 0)

    fetch_ids.wait()
    ids = ids_ref[...]
    owner = ids >> 5
    onehot = iota((OWNERS, ROWS), 0) == owner
    onehot_b = onehot.astype(BF16)
    upto = (iota((ROWS, ROWS), 0) <= iota((ROWS, ROWS), 1)).astype(BF16)
    counts = dot_nn(onehot_b, upto)
    rank = jnp.sum(jnp.where(onehot, counts, 0.0), axis=0, keepdims=True).astype(I32) - 1
    place = owner * CAP + rank
    pick = (iota((OWNERS * CAP, ROWS), 0) == place).astype(BF16)

    local = (ids - owner * CL_OWN + 1).astype(F32)
    by_rank = jnp.where(iota((128, ROWS), 0) == rank, local, 0.0).astype(BF16)
    meta_send[...] = (dot_nt(onehot_b, by_rank) - 1.0).reshape(OWNERS, 1, 128)

    fetch.wait()
    values = emb_ref[...].astype(F32)
    mean = jnp.sum(values * values, axis=1, keepdims=True) * (1.0 / D)
    scale = lax.rsqrt(mean + 1e-06) * (1.0 / math.sqrt(D))
    unit = (values * scale).astype(BF16)
    packed = dot_nn(pick, unit).astype(BF16)
    swap = swap_matrix()
    for k in range(OWNERS // 4):
        part = packed[k * BLK : (k + 1) * BLK]
        stacked = jnp.concatenate([part[:, q * QW : (q + 1) * QW] for q in range(QUARTERS)], axis=0)
        send[pl.ds(4 * k, 4)] = dot_nn(swap, stacked).astype(BF16).reshape(4, BLK, QW)

    @pl.when(is_home & (core == 1))
    def _():
        pl.semaphore_wait(barrier, OWNERS + GRP)

    @pl.when(jnp.logical_not(is_home & (core == 1)))
    def _():
        pl.semaphore_wait(barrier, OWNERS)

    plane = lax.rem(z // 2 + core, 2)

    def target(i):
        to = lax.rem(plane + i // 16, 2) * 16 + lax.rem(seat + i, 16)
        hx, hy, hz = home_of(to)
        away = lax.rem(z - hz + 4, 4)
        here = (hx == src) & (hy == y) & (away == 0)
        return to, hx, hy, hz, away, here, gray(away)

    def give_meta(i, carry):
        to, hx, hy, hz, away, here, group = target(i)
        slot = group * GRP + seat

        @pl.when(jnp.logical_not(here))
        def _():
            pltpu.make_async_remote_copy(
                meta_send.at[to], meta_recv.at[slot], meta_send_sem, meta_recv_sem,
                device_id=at(hx, hy, hz, core), device_id_type=MESH,
            ).start()

        @pl.when(here)
        def _():
            pltpu.make_async_copy(meta_send.at[to], meta_recv.at[slot], meta_recv_sem).start()

        return carry


    def give(i, carry):
        to, hx, hy, hz, away, here, group = target(i)
        slot = group * GRP + seat
        via = (away == 2) & (core == 1)

        @pl.when(via)
        def _():
            pltpu.make_async_remote_copy(
                send.at[to], recv.at[seat], send_sem, recv_sem.at[y],
                device_id=at(hx, hy, hz + 1, core), device_id_type=MESH,
            ).start()

        @pl.when(jnp.logical_not(here | via))
        def _():
            pltpu.make_async_remote_copy(
                send.at[to], recv.at[slot], send_sem, recv_sem.at[group],
                device_id=at(hx, hy, hz, core), device_id_type=MESH,
            ).start()

        @pl.when(here)
        def _():
            pltpu.make_async_copy(send.at[to], recv.at[slot], recv_sem.at[group]).start()

        return carry

    lax.fori_loop(0, 8, give, 0)
    lax.fori_loop(0, OWNERS, give_meta, 0)
    lax.fori_loop(8, OWNERS, give, 0)

    def onward(k):
        return pltpu.make_async_remote_copy(
            recv.at[pl.ds(4 * k, 4)], recv.at[pl.ds(3 * GRP + 4 * k, 4)], pass_sem, recv_sem.at[3],
            device_id=at(src, y, z - 1, core), device_id_type=MESH,
        )

    @pl.when(is_relay)
    def _():
        for k in range(4):
            block = recv.at[pl.ds(4 * k, 4)]
            pltpu.make_async_copy(block, block, recv_sem.at[k]).wait()
            onward(k).start()

    @pl.when(is_home)
    def _():
        lane_of = iota((GRP, GROWS), 1)
        spread = (div12(lane_of) == iota((GRP, GROWS), 0)).astype(BF16)
        nth_row = iota((GRP, GROWS), 0) == lane_of - div12(lane_of) * CAP
        sub = iota((GROWS, 128), 0)
        nth_col = iota((GROWS, 128), 1) == sub - div12(sub) * CAP

        pltpu.make_async_copy(meta_recv, meta_recv, meta_recv_sem).wait()
        meta_pass = pltpu.make_async_remote_copy(
            meta_recv, meta_theirs, meta_pass_sem, meta_theirs_sem,
            device_id=partner, device_id_type=MESH,
        )
        meta_pass.start()

        def down(ref, g):
            ids_g = ref[pl.ds(g * GRP, GRP)].reshape(GRP, 128).astype(BF16)
            wide = dot_tn(spread, ids_g)
            return ids_g, jnp.sum(jnp.where(nth_col, wide, 0.0), axis=1, keepdims=True)

        along = []
        for g in range(NGRP):
            ids_g, col_g = down(meta_recv, g)
            id_col[0, g * GROWS : (g + 1) * GROWS] = col_g
            wide = dot_tn(ids_g, spread)[:GRP]
            along.append(jnp.sum(jnp.where(nth_row, wide, 0.0), axis=0, keepdims=True))
        along = jnp.concatenate(along, axis=1)
        meta_pass.wait_recv()
        for g in range(NGRP):
            id_col[1, g * GROWS : (g + 1) * GROWS] = down(meta_theirs, g)[1]

        def passing(g):
            part = pl.ds(g * GROWS, GROWS)
            return pltpu.make_async_remote_copy(
                rows.at[part], theirs.at[part], pass_sem, theirs_sem.at[g // 2],
                device_id=partner, device_id_type=MESH,
            )

        def turn(g):
            block = recv.at[pl.ds(g * GRP, GRP)]
            pltpu.make_async_copy(block, block, recv_sem.at[g]).wait()
            for k in range(GRP // 4):
                four = recv[pl.ds(g * GRP + 4 * k, 4)].reshape(GROWS, QW)
                turned = dot_nn(swap, four).astype(BF16)
                first = g * GROWS + k * BLK
                for q in range(QUARTERS):
                    rows[first : first + BLK, q * QW : (q + 1) * QW] = turned[q * BLK : (q + 1) * BLK]
            passing(g).start()

        def top(ref, side, down_at, along_at):
            mine = rows[along_at : along_at + HALF, :]
            scores = dot_nt(ref[down_at : down_at + HALF, :], mine)
            keep = id_col[side, down_at : down_at + HALF] == along[:, along_at : along_at + HALF]
            if side == 0 and down_at == along_at:
                keep &= iota((HALF, HALF), 0) != iota((HALF, HALF), 1)
            return jnp.max(jnp.where(keep, scores, -1.0), axis=0, keepdims=True)

        def arrived(half):
            part = theirs.at[pl.ds(half * HALF, HALF)]
            pltpu.make_async_copy(part, part, theirs_sem.at[half]).wait()

        def give_back(g, found):
            best[g, :, :GROWS] = found
            for to in range(GRP):
                device = at(to % 4, to // 4, lax.rem(z + gray(g), 4), core)

                def one(device=device):
                    pltpu.make_async_remote_copy(
                        best.at[g], back.at[shard], back_send_sem, back_sem,
                        device_id=device, device_id_type=MESH,
                    ).start()

                if g:
                    one()
                else:
                    pl.when(to != seat)(one)
            if g == 0:
                pltpu.make_async_copy(best.at[0], back.at[shard], back_sem).start()

        turn(0)
        turn(1)
        first = top(rows, 0, 0, 0)
        arrived(0)
        first = jnp.maximum(first, top(theirs, 1, 0, 0))
        turn(2)
        turn(3)
        second = jnp.maximum(top(rows, 0, 0, HALF), top(rows, 0, HALF, HALF))
        second = jnp.maximum(second, top(theirs, 1, 0, HALF))
        first = jnp.maximum(first, top(rows, 0, HALF, 0))
        arrived(1)
        first = jnp.maximum(jnp.maximum(first, top(theirs, 1, HALF, 0)), -1.0)
        give_back(0, first[:, :GROWS])
        give_back(1, first[:, GROWS:])
        second = jnp.maximum(jnp.maximum(second, top(theirs, 1, HALF, HALF)), -1.0)
        give_back(2, second[:, :GROWS])
        give_back(3, second[:, GROWS:])

    pltpu.make_async_copy(back, back, back_sem).wait()
    got = back[...].reshape(OWNERS, RETW)
    high = got.astype(BF16)
    rest = got - high.astype(F32)
    mid = rest.astype(BF16)
    low = (rest - mid.astype(F32)).astype(BF16)
    wide = dot_tn(high, onehot_b) + dot_tn(mid, onehot_b) + dot_tn(low, onehot_b)
    lane = seat * CAP + rank
    out_ref[...] = jnp.sum(jnp.where(iota((RETW, ROWS), 0) == lane, wide, 0.0), axis=0, keepdims=True)

    @pl.when(is_home)
    def _():
        part = send.at[pl.ds(0, OWNERS - 1)]
        pltpu.make_async_copy(part, part, send_sem).wait()
        part = meta_send.at[pl.ds(0, OWNERS - 1)]
        pltpu.make_async_copy(part, part, meta_send_sem).wait()
        pltpu.make_async_copy(meta_recv, meta_recv, meta_pass_sem).wait()
        pltpu.make_async_copy(rows, rows, pass_sem).wait()
        pltpu.make_async_copy(back, back, back_send_sem).wait()
        part = back.at[pl.ds(0, OWNERS - 1)]
        pltpu.make_async_copy(part, part, back_send_sem).wait()

    @pl.when(jnp.logical_not(is_home))
    def _():
        pltpu.make_async_copy(send, send, send_sem).wait()
        pltpu.make_async_copy(meta_send, meta_send, meta_send_sem).wait()

    @pl.when(is_relay)
    def _():
        part = recv.at[pl.ds(0, GRP)]
        pltpu.make_async_copy(part, part, pass_sem).wait()


def shards(embeddings, cluster_ids):
    dma = pltpu.SemaphoreType.DMA
    out = pl.pallas_call(
        kernel,
        out_shape=jax.ShapeDtypeStruct((1, ROWS), F32),
        in_specs=[pl.BlockSpec(memory_space=pltpu.HBM)] * 2,
        out_specs=pl.BlockSpec(memory_space=pltpu.VMEM),
        scratch_shapes=[
            pltpu.VMEM((ROWS, D), BF16),
            pltpu.VMEM((1, ROWS), I32),
            pltpu.VMEM((OWNERS, BLK, QW), BF16),
            pltpu.VMEM((OWNERS, 1, 128), F32),
            pltpu.VMEM((SLOTS, BLK, QW), BF16),
            pltpu.VMEM((SLOTS, 1, 128), F32),
            pltpu.VMEM((HROWS, D), BF16),
            pltpu.VMEM((HROWS, D), BF16),
            pltpu.VMEM((SLOTS, 1, 128), F32),
            pltpu.VMEM((2, HROWS, 1), F32),
            pltpu.VMEM((NGRP, 1, RETW), F32),
            pltpu.VMEM((OWNERS, 1, RETW), F32),
            dma, dma, dma, dma, dma((NGRP,)), dma, dma, dma((2,)), dma, dma, dma, dma,
        ],
        compiler_params=pltpu.CompilerParams(
            collective_id=0, has_side_effects=True, vmem_limit_bytes=60 << 20
        ),
    )(embeddings, cluster_ids.reshape(1, ROWS))
    return out.reshape(ROWS)


def solution(mesh):
    in_specs = (P(("src", "own"), None), P(("src", "own")))
    out_specs = P(("src", "own"))
    return jax.shard_map(shards, mesh=mesh, in_specs=in_specs, out_specs=out_specs, check_vma=False)
```

```python
import functools
import math

import jax
import jax.numpy as jnp
from jax import lax
from jax.experimental import pallas as pl
from jax.experimental.pallas import tpu as pltpu
from jax.sharding import PartitionSpec as P

MESH = pl.DeviceIdType.MESH
F32, BF16, I32 = jnp.float32, jnp.bfloat16, jnp.int32

D = 1024
ROWS = 192
CAP = 12
OWNERS = 32
SLOTS = 64
CL_OWN = 32
QUARTERS = 4
QW = D // QUARTERS
BLK = QUARTERS * CAP
GRP = 16
NGRP = SLOTS // GRP
GROWS = GRP * CAP
HROWS = SLOTS * CAP
HALF = HROWS // 2
RETW = 256


def home_of(owner):
    return lax.rem(owner, 4), lax.rem(owner // 4, 4), (owner // 16) * 2


def gray(v):
    return v + (v // 2) * (1 - 2 * lax.rem(v, 2))


def at(x, y, z, core):
    return x, y * 8 + z * 2 + core


def div12(v):
    return (v * 5462) >> 16


def dot_nn(a, b):
    return lax.dot_general(a, b, (((1,), (0,)), ((), ())), preferred_element_type=F32)


def dot_nt(a, b):
    return lax.dot_general(a, b, (((1,), (1,)), ((), ())), preferred_element_type=F32)


def dot_tn(a, b):
    return lax.dot_general(a, b, (((0,), (0,)), ((), ())), preferred_element_type=F32)


def iota(shape, dim):
    return lax.broadcasted_iota(I32, shape, dim)


def swap_matrix():
    i, j = iota((GROWS, GROWS), 0), iota((GROWS, GROWS), 1)
    ab = div12(i)
    a, b = ab >> 2, ab & 3
    return (j == b * BLK + a * CAP + (i - ab * CAP)).astype(BF16)


def kernel(
    emb_hbm, ids_hbm, out_ref,
    emb_ref, ids_ref, send, meta_send, recv, meta_recv, rows, theirs, meta_theirs, id_col, best, back,
    emb_sem, ids_sem, send_sem, meta_send_sem, recv_sem, meta_recv_sem, pass_sem, theirs_sem,
    meta_pass_sem, meta_theirs_sem, back_send_sem, back_sem,
):
    src, own = lax.axis_index("src"), lax.axis_index("own")
    y, z, core = own // 8, lax.rem(own // 2, 4), lax.rem(own, 2)
    is_home, shard = lax.rem(z, 2) == 0, (z // 2) * 16 + y * 4 + src
    is_relay = (lax.rem(z, 2) == 1) & (core == 1)
    seat = y * 4 + src
    partner = (src, own + 1 - 2 * core)

    barrier = pltpu.get_barrier_semaphore()
    fetch = pltpu.make_async_copy(emb_hbm, emb_ref, emb_sem)
    fetch_ids = pltpu.make_async_copy(ids_hbm, ids_ref, ids_sem)
    fetch_ids.start()
    fetch.start()

    @pl.when(is_home)
    def _():
        pl.semaphore_signal(barrier, inc=1, device_id=partner, device_id_type=MESH)

        def greet(i, carry):
            to = lax.rem(z * 16 + seat + i, SLOTS)
            device = at(lax.rem(to, 4), lax.rem(to // 4, 4), to // 16, core)
            pl.semaphore_signal(barrier, inc=1, device_id=device, device_id_type=MESH)
            return carry

        lax.fori_loop(1, SLOTS, greet, 0)

    @pl.when(is_relay)
    def _():
        def greet(i, carry):
            device = at(lax.rem(i, 4), i // 4, lax.rem(z + 1, 4), core)
            pl.semaphore_signal(barrier, inc=1, device_id=device, device_id_type=MESH)
            return carry

        lax.fori_loop(0, GRP, greet, 0)

    fetch_ids.wait()
    ids = ids_ref[...]
    owner = ids >> 5
    onehot = iota((OWNERS, ROWS), 0) == owner
    onehot_b = onehot.astype(BF16)
    upto = (iota((ROWS, ROWS), 0) <= iota((ROWS, ROWS), 1)).astype(BF16)
    counts = dot_nn(onehot_b, upto)
    rank = jnp.sum(jnp.where(onehot, counts, 0.0), axis=0, keepdims=True).astype(I32) - 1
    place = owner * CAP + rank
    pick = (iota((OWNERS * CAP, ROWS), 0) == place).astype(BF16)

    local = (ids - owner * CL_OWN + 1).astype(F32)
    by_rank = jnp.where(iota((128, ROWS), 0) == rank, local, 0.0).astype(BF16)
    meta_send[...] = (dot_nt(onehot_b, by_rank) - 1.0).reshape(OWNERS, 1, 128)

    fetch.wait()
    values = emb_ref[...].astype(F32)
    mean = jnp.sum(values * values, axis=1, keepdims=True) * (1.0 / D)
    scale = lax.rsqrt(mean + 1e-06) * (1.0 / math.sqrt(D))
    unit = (values * scale).astype(BF16)
    packed = dot_nn(pick, unit).astype(BF16)
    swap = swap_matrix()
    for k in range(OWNERS // 4):
        part = packed[k * BLK : (k + 1) * BLK]
        stacked = jnp.concatenate([part[:, q * QW : (q + 1) * QW] for q in range(QUARTERS)], axis=0)
        send[pl.ds(4 * k, 4)] = dot_nn(swap, stacked).astype(BF16).reshape(4, BLK, QW)

    @pl.when(is_home & (core == 1))
    def _():
        pl.semaphore_wait(barrier, OWNERS + GRP)

    @pl.when(jnp.logical_not(is_home & (core == 1)))
    def _():
        pl.semaphore_wait(barrier, OWNERS)

    plane = lax.rem(z // 2 + core, 2)

    def send_one(source, landed, device, sent, arrived, here):
        def away():
            pltpu.make_async_remote_copy(
                source, landed, sent, arrived, device_id=device, device_id_type=MESH
            ).start()

        if here is None:
            away()
        else:
            pl.when(jnp.logical_not(here))(away)
            pl.when(here)(lambda: pltpu.make_async_copy(source, landed, arrived).start())

    def half(p):
        hz = 2 * lax.rem(plane + p, 2)
        above = lax.rem(z - hz + 4, 4)
        group = gray(above)
        via = core * (above // 2) * (1 - lax.rem(above, 2))
        landing = seat + GRP * group * (1 - via)
        signal = group + via * (y - group)

        def place(j):
            if isinstance(j, int):
                dx, dy = (0, 1, 3, 2)[j % 4], (0, 1, 3, 2)[j // 4]
            else:
                dx, dy = gray(lax.rem(j, 4)), gray(j // 4)
            hx, hy = lax.rem(src + dx, 4), lax.rem(y + dy, 4)
            here = (above == 0) if isinstance(j, int) and j == 0 else None
            return hx, hy, 8 * hz + 4 * hy + hx, here

        def give(j, carry):
            hx, hy, to, here = place(j)
            send_one(
                send.at[to], recv.at[landing], at(hx, hy, hz + via, core), send_sem, recv_sem.at[signal], here
            )
            return carry

        def give_meta(j, carry):
            hx, hy, to, here = place(j)
            send_one(
                meta_send.at[to], meta_recv.at[GRP * group + seat], at(hx, hy, hz, core),
                meta_send_sem, meta_recv_sem, here,
            )
            return carry

        return give, give_meta

    def run(f, first, last):
        if first == 0:
            f(0, 0)
        lax.fori_loop(max(first, 1), last, f, 0, unroll=False)

    rows_a, ids_a = half(0)
    rows_b, ids_b = half(1)
    run(rows_a, 0, 8)
    run(ids_a, 0, GRP)
    run(ids_b, 0, GRP)
    run(rows_a, 8, GRP)
    run(rows_b, 0, GRP)

    def onward(k):
        return pltpu.make_async_remote_copy(
            recv.at[pl.ds(4 * k, 4)], recv.at[pl.ds(3 * GRP + 4 * k, 4)], pass_sem, recv_sem.at[3],
            device_id=at(src, y, z - 1, core), device_id_type=MESH,
        )

    @pl.when(is_relay)
    def _():
        for k in range(4):
            block = recv.at[pl.ds(4 * k, 4)]
            pltpu.make_async_copy(block, block, recv_sem.at[k]).wait()
            onward(k).start()

    @pl.when(is_home)
    def _():
        lane_of = iota((GRP, GROWS), 1)
        spread = (div12(lane_of) == iota((GRP, GROWS), 0)).astype(BF16)
        nth_row = iota((GRP, GROWS), 0) == lane_of - div12(lane_of) * CAP
        sub = iota((GROWS, 128), 0)
        nth_col = iota((GROWS, 128), 1) == sub - div12(sub) * CAP

        pltpu.make_async_copy(meta_recv, meta_recv, meta_recv_sem).wait()
        meta_pass = pltpu.make_async_remote_copy(
            meta_recv, meta_theirs, meta_pass_sem, meta_theirs_sem,
            device_id=partner, device_id_type=MESH,
        )
        meta_pass.start()

        def down(ref, g):
            ids_g = ref[pl.ds(g * GRP, GRP)].reshape(GRP, 128).astype(BF16)
            wide = dot_tn(spread, ids_g)
            return ids_g, jnp.sum(jnp.where(nth_col, wide, 0.0), axis=1, keepdims=True)

        along = []
        for g in range(NGRP):
            ids_g, col_g = down(meta_recv, g)
            id_col[0, g * GROWS : (g + 1) * GROWS] = col_g
            wide = dot_tn(ids_g, spread)[:GRP]
            along.append(jnp.sum(jnp.where(nth_row, wide, 0.0), axis=0, keepdims=True))
        along = jnp.concatenate(along, axis=1)
        meta_pass.wait_recv()
        for g in range(NGRP):
            id_col[1, g * GROWS : (g + 1) * GROWS] = down(meta_theirs, g)[1]

        def passing(g):
            part = pl.ds(g * GROWS, GROWS)
            return pltpu.make_async_remote_copy(
                rows.at[part], theirs.at[part], pass_sem, theirs_sem.at[g // 2],
                device_id=partner, device_id_type=MESH,
            )

        def turn(g):
            block = recv.at[pl.ds(g * GRP, GRP)]
            pltpu.make_async_copy(block, block, recv_sem.at[g]).wait()
            for k in range(GRP // 4):
                four = recv[pl.ds(g * GRP + 4 * k, 4)].reshape(GROWS, QW)
                turned = dot_nn(swap, four).astype(BF16)
                first = g * GROWS + k * BLK
                for q in range(QUARTERS):
                    rows[first : first + BLK, q * QW : (q + 1) * QW] = turned[q * BLK : (q + 1) * BLK]
            passing(g).start()

        def top(ref, side, down_at, along_at):
            mine = rows[along_at : along_at + HALF, :]
            scores = dot_nt(ref[down_at : down_at + HALF, :], mine)
            keep = id_col[side, down_at : down_at + HALF] == along[:, along_at : along_at + HALF]
            if side == 0 and down_at == along_at:
                keep &= iota((HALF, HALF), 0) != iota((HALF, HALF), 1)
            return jnp.max(jnp.where(keep, scores, -1.0), axis=0, keepdims=True)

        def arrived(half):
            part = theirs.at[pl.ds(half * HALF, HALF)]
            pltpu.make_async_copy(part, part, theirs_sem.at[half]).wait()

        def give_back(g, found):
            best[g, :, :GROWS] = found
            for to in range(GRP):
                device = at(to % 4, to // 4, lax.rem(z + (0, 1, 3, 2)[g], 4), core)

                def one(device=device):
                    pltpu.make_async_remote_copy(
                        best.at[g], back.at[shard], back_send_sem, back_sem,
                        device_id=device, device_id_type=MESH,
                    ).start()

                if g:
                    one()
                else:
                    pl.when(to != seat)(one)
            if g == 0:
                pltpu.make_async_copy(best.at[0], back.at[shard], back_sem).start()

        turn(0)
        turn(1)
        first = top(rows, 0, 0, 0)
        arrived(0)
        first = jnp.maximum(first, top(theirs, 1, 0, 0))
        turn(2)
        turn(3)
        second = jnp.maximum(top(rows, 0, 0, HALF), top(rows, 0, HALF, HALF))
        second = jnp.maximum(second, top(theirs, 1, 0, HALF))
        first = jnp.maximum(first, top(rows, 0, HALF, 0))
        arrived(1)
        first = jnp.maximum(jnp.maximum(first, top(theirs, 1, HALF, 0)), -1.0)
        give_back(0, first[:, :GROWS])
        give_back(1, first[:, GROWS:])
        second = jnp.maximum(jnp.maximum(second, top(theirs, 1, HALF, HALF)), -1.0)
        give_back(2, second[:, :GROWS])
        give_back(3, second[:, GROWS:])

    pltpu.make_async_copy(back, back, back_sem).wait()
    got = back[...].reshape(OWNERS, RETW)
    high = got.astype(BF16)
    rest = got - high.astype(F32)
    mid = rest.astype(BF16)
    low = (rest - mid.astype(F32)).astype(BF16)
    wide = dot_tn(high, onehot_b) + dot_tn(mid, onehot_b) + dot_tn(low, onehot_b)
    lane = seat * CAP + rank
    out_ref[...] = jnp.sum(jnp.where(iota((RETW, ROWS), 0) == lane, wide, 0.0), axis=0, keepdims=True)

    @pl.when(is_home)
    def _():
        part = send.at[pl.ds(0, OWNERS - 1)]
        pltpu.make_async_copy(part, part, send_sem).wait()
        part = meta_send.at[pl.ds(0, OWNERS - 1)]
        pltpu.make_async_copy(part, part, meta_send_sem).wait()
        pltpu.make_async_copy(meta_recv, meta_recv, meta_pass_sem).wait()
        pltpu.make_async_copy(rows, rows, pass_sem).wait()
        pltpu.make_async_copy(back, back, back_send_sem).wait()
        part = back.at[pl.ds(0, OWNERS - 1)]
        pltpu.make_async_copy(part, part, back_send_sem).wait()

    @pl.when(jnp.logical_not(is_home))
    def _():
        pltpu.make_async_copy(send, send, send_sem).wait()
        pltpu.make_async_copy(meta_send, meta_send, meta_send_sem).wait()

    @pl.when(is_relay)
    def _():
        part = recv.at[pl.ds(0, GRP)]
        pltpu.make_async_copy(part, part, pass_sem).wait()


def shards(embeddings, cluster_ids):
    dma = pltpu.SemaphoreType.DMA
    out = pl.pallas_call(
        kernel,
        out_shape=jax.ShapeDtypeStruct((1, ROWS), F32),
        in_specs=[pl.BlockSpec(memory_space=pltpu.HBM)] * 2,
        out_specs=pl.BlockSpec(memory_space=pltpu.VMEM),
        scratch_shapes=[
            pltpu.VMEM((ROWS, D), BF16),
            pltpu.VMEM((1, ROWS), I32),
            pltpu.VMEM((OWNERS, BLK, QW), BF16),
            pltpu.VMEM((OWNERS, 1, 128), F32),
            pltpu.VMEM((SLOTS, BLK, QW), BF16),
            pltpu.VMEM((SLOTS, 1, 128), F32),
            pltpu.VMEM((HROWS, D), BF16),
            pltpu.VMEM((HROWS, D), BF16),
            pltpu.VMEM((SLOTS, 1, 128), F32),
            pltpu.VMEM((2, HROWS, 1), F32),
            pltpu.VMEM((NGRP, 1, RETW), F32),
            pltpu.VMEM((OWNERS, 1, RETW), F32),
            dma, dma, dma, dma, dma((NGRP,)), dma, dma, dma((2,)), dma, dma, dma, dma,
        ],
        compiler_params=pltpu.CompilerParams(
            collective_id=0, has_side_effects=True, vmem_limit_bytes=60 << 20
        ),
    )(embeddings, cluster_ids.reshape(1, ROWS))
    return out.reshape(ROWS)


def solution(mesh):
    in_specs = (P(("src", "own"), None), P(("src", "own")))
    out_specs = P(("src", "own"))
    return jax.shard_map(shards, mesh=mesh, in_specs=in_specs, out_specs=out_specs, check_vma=False)
```

```python
import functools
import math

import jax
import jax.numpy as jnp
from jax import lax
from jax.experimental import pallas as pl
from jax.experimental.pallas import tpu as pltpu
from jax.sharding import PartitionSpec as P

MESH = pl.DeviceIdType.MESH
F32, BF16, I32 = jnp.float32, jnp.bfloat16, jnp.int32

D = 1024
ROWS = 192
CAP = 12
OWNERS = 32
SLOTS = 64
CL_OWN = 32
QUARTERS = 4
QW = D // QUARTERS
BLK = QUARTERS * CAP
GRP = 16
NGRP = SLOTS // GRP
GROWS = GRP * CAP
HROWS = SLOTS * CAP
HALF = HROWS // 2
RETW = 256


def home_of(owner):
    return lax.rem(owner, 4), lax.rem(owner // 4, 4), (owner // 16) * 2


def gray(v):
    return v + (v // 2) * (1 - 2 * lax.rem(v, 2))


def at(x, y, z, core):
    return x, y * 8 + z * 2 + core


def div12(v):
    return (v * 5462) >> 16


def dot_nn(a, b):
    return lax.dot_general(a, b, (((1,), (0,)), ((), ())), preferred_element_type=F32)


def dot_nt(a, b):
    return lax.dot_general(a, b, (((1,), (1,)), ((), ())), preferred_element_type=F32)


def dot_tn(a, b):
    return lax.dot_general(a, b, (((0,), (0,)), ((), ())), preferred_element_type=F32)


def iota(shape, dim):
    return lax.broadcasted_iota(I32, shape, dim)


def swap_matrix():
    i, j = iota((GROWS, GROWS), 0), iota((GROWS, GROWS), 1)
    ab = div12(i)
    a, b = ab >> 2, ab & 3
    return (j == b * BLK + a * CAP + (i - ab * CAP)).astype(BF16)


def kernel(
    emb_hbm, ids_hbm, out_ref,
    emb_ref, ids_ref, send, meta_send, recv, meta_recv, rows, theirs, meta_theirs, id_col, best, back,
    emb_sem, ids_sem, send_sem, meta_send_sem, recv_sem, meta_recv_sem, pass_sem, theirs_sem,
    meta_pass_sem, meta_theirs_sem, back_send_sem, back_sem,
):
    src, own = lax.axis_index("src"), lax.axis_index("own")
    y, z, core = own // 8, lax.rem(own // 2, 4), lax.rem(own, 2)
    is_home, shard = lax.rem(z, 2) == 0, (z // 2) * 16 + y * 4 + src
    is_relay = (lax.rem(z, 2) == 1) & (core == 1)
    seat = y * 4 + src
    partner = (src, own + 1 - 2 * core)

    barrier = pltpu.get_barrier_semaphore()
    fetch = pltpu.make_async_copy(emb_hbm, emb_ref, emb_sem)
    fetch_ids = pltpu.make_async_copy(ids_hbm, ids_ref, ids_sem)
    fetch_ids.start()
    fetch.start()

    @pl.when(is_home)
    def _():
        pl.semaphore_signal(barrier, inc=1, device_id=partner, device_id_type=MESH)

        def greet(i, carry):
            to = lax.rem(z * 16 + seat + i, SLOTS)
            device = at(lax.rem(to, 4), lax.rem(to // 4, 4), to // 16, core)
            pl.semaphore_signal(barrier, inc=1, device_id=device, device_id_type=MESH)
            return carry

        lax.fori_loop(1, SLOTS, greet, 0)

    @pl.when(is_relay)
    def _():
        def greet(i, carry):
            device = at(lax.rem(i, 4), i // 4, lax.rem(z + 1, 4), core)
            pl.semaphore_signal(barrier, inc=1, device_id=device, device_id_type=MESH)
            return carry

        lax.fori_loop(0, GRP, greet, 0)

    fetch_ids.wait()
    ids = ids_ref[...]
    owner = ids >> 5
    onehot = iota((OWNERS, ROWS), 0) == owner
    onehot_b = onehot.astype(BF16)
    upto = (iota((ROWS, ROWS), 0) <= iota((ROWS, ROWS), 1)).astype(BF16)
    counts = dot_nn(onehot_b, upto)
    rank = jnp.sum(jnp.where(onehot, counts, 0.0), axis=0, keepdims=True).astype(I32) - 1
    place = owner * CAP + rank
    pick = (iota((OWNERS * CAP, ROWS), 0) == place).astype(BF16)

    local = (ids - owner * CL_OWN + 1).astype(F32)
    by_rank = jnp.where(iota((128, ROWS), 0) == rank, local, 0.0).astype(BF16)
    meta_send[...] = (dot_nt(onehot_b, by_rank) - 1.0).reshape(OWNERS, 1, 128)

    fetch.wait()
    values = emb_ref[...].astype(F32)
    mean = jnp.sum(values * values, axis=1, keepdims=True) * (1.0 / D)
    scale = lax.rsqrt(mean + 1e-06) * (1.0 / math.sqrt(D))
    unit = (values * scale).astype(BF16)
    packed = dot_nn(pick, unit).astype(BF16)
    swap = swap_matrix()
    for k in range(OWNERS // 4):
        part = packed[k * BLK : (k + 1) * BLK]
        stacked = jnp.concatenate([part[:, q * QW : (q + 1) * QW] for q in range(QUARTERS)], axis=0)
        send[pl.ds(4 * k, 4)] = dot_nn(swap, stacked).astype(BF16).reshape(4, BLK, QW)

    @pl.when(is_home & (core == 1))
    def _():
        pl.semaphore_wait(barrier, OWNERS + GRP)

    @pl.when(jnp.logical_not(is_home & (core == 1)))
    def _():
        pl.semaphore_wait(barrier, OWNERS)

    plane = lax.rem(z // 2 + core, 2)

    def send_one(source, landed, device, sent, arrived, here):
        def away():
            pltpu.make_async_remote_copy(
                source, landed, sent, arrived, device_id=device, device_id_type=MESH
            ).start()

        if here is None:
            away()
        else:
            pl.when(jnp.logical_not(here))(away)
            pl.when(here)(lambda: pltpu.make_async_copy(source, landed, arrived).start())

    def half(p):
        hz = 2 * lax.rem(plane + p, 2)
        above = lax.rem(z - hz + 4, 4)
        group = gray(above)
        via = core * (above // 2) * (1 - lax.rem(above, 2))
        landing = seat + GRP * group * (1 - via)
        signal = group + via * (y - group)

        def place(j):
            if isinstance(j, int):
                dx, dy = (0, 1, 3, 2)[j % 4], (0, 1, 3, 2)[j // 4]
            else:
                dx, dy = gray(lax.rem(j, 4)), gray(j // 4)
            hx, hy = lax.rem(src + dx, 4), lax.rem(y + dy, 4)
            here = (above == 0) if isinstance(j, int) and j == 0 else None
            return hx, hy, 8 * hz + 4 * hy + hx, here

        def give(j, carry):
            hx, hy, to, here = place(j)
            send_one(
                send.at[to], recv.at[landing], at(hx, hy, hz + via, core), send_sem, recv_sem.at[signal], here
            )
            return carry

        def give_meta(j, carry):
            hx, hy, to, here = place(j)
            send_one(
                meta_send.at[to], meta_recv.at[GRP * group + seat], at(hx, hy, hz, core),
                meta_send_sem, meta_recv_sem, here,
            )
            return carry

        return give, give_meta

    def run(f, first, last):
        if first == 0:
            f(0, 0)
        lax.fori_loop(max(first, 1), last, f, 0, unroll=False)

    rows_a, ids_a = half(0)
    rows_b, ids_b = half(1)
    run(rows_a, 0, 8)
    run(ids_a, 0, GRP)
    run(ids_b, 0, GRP)
    run(rows_a, 8, GRP)
    run(rows_b, 0, GRP)

    def onward(k):
        return pltpu.make_async_remote_copy(
            recv.at[pl.ds(4 * k, 4)], recv.at[pl.ds(3 * GRP + 4 * k, 4)], pass_sem, recv_sem.at[3],
            device_id=at(src, y, z - 1, core), device_id_type=MESH,
        )

    @pl.when(is_relay)
    def _():
        for k in range(4):
            block = recv.at[pl.ds(4 * k, 4)]
            pltpu.make_async_copy(block, block, recv_sem.at[k]).wait()
            onward(k).start()

    @pl.when(is_home)
    def _():
        lane_of = iota((GRP, GROWS), 1)
        spread = (div12(lane_of) == iota((GRP, GROWS), 0)).astype(BF16)
        nth_row = iota((GRP, GROWS), 0) == lane_of - div12(lane_of) * CAP
        sub = iota((GROWS, 128), 0)
        nth_col = iota((GROWS, 128), 1) == sub - div12(sub) * CAP

        pltpu.make_async_copy(meta_recv, meta_recv, meta_recv_sem).wait()
        meta_pass = pltpu.make_async_remote_copy(
            meta_recv, meta_theirs, meta_pass_sem, meta_theirs_sem,
            device_id=partner, device_id_type=MESH,
        )
        meta_pass.start()

        def down(ref, g):
            ids_g = ref[pl.ds(g * GRP, GRP)].reshape(GRP, 128).astype(BF16)
            wide = dot_tn(spread, ids_g)
            return ids_g, jnp.sum(jnp.where(nth_col, wide, 0.0), axis=1, keepdims=True)

        along = []
        for g in range(NGRP):
            ids_g, col_g = down(meta_recv, g)
            id_col[0, g * GROWS : (g + 1) * GROWS] = col_g
            wide = dot_tn(ids_g, spread)[:GRP]
            along.append(jnp.sum(jnp.where(nth_row, wide, 0.0), axis=0, keepdims=True))
        along = jnp.concatenate(along, axis=1)
        meta_pass.wait_recv()
        for g in range(NGRP):
            id_col[1, g * GROWS : (g + 1) * GROWS] = down(meta_theirs, g)[1]

        def passing(g):
            part = pl.ds(g * GROWS, GROWS)
            return pltpu.make_async_remote_copy(
                rows.at[part], theirs.at[part], pass_sem, theirs_sem.at[g // 2],
                device_id=partner, device_id_type=MESH,
            )

        def turn(g):
            block = recv.at[pl.ds(g * GRP, GRP)]
            pltpu.make_async_copy(block, block, recv_sem.at[g]).wait()
            for k in range(GRP // 4):
                four = recv[pl.ds(g * GRP + 4 * k, 4)].reshape(GROWS, QW)
                turned = dot_nn(swap, four).astype(BF16)
                first = g * GROWS + k * BLK
                for q in range(QUARTERS):
                    rows[first : first + BLK, q * QW : (q + 1) * QW] = turned[q * BLK : (q + 1) * BLK]
            passing(g).start()

        def top(ref, side, down_at, along_at):
            mine = rows[along_at : along_at + HALF, :]
            scores = dot_nt(ref[down_at : down_at + HALF, :], mine)
            keep = id_col[side, down_at : down_at + HALF] == along[:, along_at : along_at + HALF]
            if side == 0 and down_at == along_at:
                keep &= iota((HALF, HALF), 0) != iota((HALF, HALF), 1)
            return jnp.max(jnp.where(keep, scores, -1.0), axis=0, keepdims=True)

        def arrived(half):
            part = theirs.at[pl.ds(half * HALF, HALF)]
            pltpu.make_async_copy(part, part, theirs_sem.at[half]).wait()

        def give_back(g, found):
            best[g, :, :GROWS] = found
            for to in range(GRP):
                device = at(to % 4, to // 4, lax.rem(z + (0, 1, 3, 2)[g], 4), core)

                def one(device=device):
                    pltpu.make_async_remote_copy(
                        best.at[g], back.at[shard], back_send_sem, back_sem,
                        device_id=device, device_id_type=MESH,
                    ).start()

                if g:
                    one()
                else:
                    pl.when(to != seat)(one)
            if g == 0:
                pltpu.make_async_copy(best.at[0], back.at[shard], back_sem).start()

        turn(0)
        turn(1)
        first = top(rows, 0, 0, 0)
        arrived(0)
        first = jnp.maximum(first, top(theirs, 1, 0, 0))
        turn(2)
        turn(3)
        second = jnp.maximum(top(rows, 0, 0, HALF), top(rows, 0, HALF, HALF))
        second = jnp.maximum(second, top(theirs, 1, 0, HALF))
        first = jnp.maximum(first, top(rows, 0, HALF, 0))
        arrived(1)
        second = jnp.maximum(jnp.maximum(second, top(theirs, 1, HALF, HALF)), -1.0)
        give_back(3, second[:, GROWS:])
        give_back(2, second[:, :GROWS])
        first = jnp.maximum(jnp.maximum(first, top(theirs, 1, HALF, 0)), -1.0)
        give_back(1, first[:, GROWS:])
        give_back(0, first[:, :GROWS])

    pltpu.make_async_copy(back, back, back_sem).wait()
    got = back[...].reshape(OWNERS, RETW)
    high = got.astype(BF16)
    rest = got - high.astype(F32)
    mid = rest.astype(BF16)
    low = (rest - mid.astype(F32)).astype(BF16)
    wide = dot_tn(high, onehot_b) + dot_tn(mid, onehot_b) + dot_tn(low, onehot_b)
    lane = seat * CAP + rank
    out_ref[...] = jnp.sum(jnp.where(iota((RETW, ROWS), 0) == lane, wide, 0.0), axis=0, keepdims=True)

    @pl.when(is_home)
    def _():
        part = send.at[pl.ds(0, OWNERS - 1)]
        pltpu.make_async_copy(part, part, send_sem).wait()
        part = meta_send.at[pl.ds(0, OWNERS - 1)]
        pltpu.make_async_copy(part, part, meta_send_sem).wait()
        pltpu.make_async_copy(meta_recv, meta_recv, meta_pass_sem).wait()
        pltpu.make_async_copy(rows, rows, pass_sem).wait()
        pltpu.make_async_copy(back, back, back_send_sem).wait()
        part = back.at[pl.ds(0, OWNERS - 1)]
        pltpu.make_async_copy(part, part, back_send_sem).wait()

    @pl.when(jnp.logical_not(is_home))
    def _():
        pltpu.make_async_copy(send, send, send_sem).wait()
        pltpu.make_async_copy(meta_send, meta_send, meta_send_sem).wait()

    @pl.when(is_relay)
    def _():
        part = recv.at[pl.ds(0, GRP)]
        pltpu.make_async_copy(part, part, pass_sem).wait()


def shards(embeddings, cluster_ids):
    dma = pltpu.SemaphoreType.DMA
    out = pl.pallas_call(
        kernel,
        out_shape=jax.ShapeDtypeStruct((1, ROWS), F32),
        in_specs=[pl.BlockSpec(memory_space=pltpu.HBM)] * 2,
        out_specs=pl.BlockSpec(memory_space=pltpu.VMEM),
        scratch_shapes=[
            pltpu.VMEM((ROWS, D), BF16),
            pltpu.VMEM((1, ROWS), I32),
            pltpu.VMEM((OWNERS, BLK, QW), BF16),
            pltpu.VMEM((OWNERS, 1, 128), F32),
            pltpu.VMEM((SLOTS, BLK, QW), BF16),
            pltpu.VMEM((SLOTS, 1, 128), F32),
            pltpu.VMEM((HROWS, D), BF16),
            pltpu.VMEM((HROWS, D), BF16),
            pltpu.VMEM((SLOTS, 1, 128), F32),
            pltpu.VMEM((2, HROWS, 1), F32),
            pltpu.VMEM((NGRP, 1, RETW), F32),
            pltpu.VMEM((OWNERS, 1, RETW), F32),
            dma, dma, dma, dma, dma((NGRP,)), dma, dma, dma((2,)), dma, dma, dma, dma,
        ],
        compiler_params=pltpu.CompilerParams(
            collective_id=0, has_side_effects=True, vmem_limit_bytes=60 << 20
        ),
    )(embeddings, cluster_ids.reshape(1, ROWS))
    return out.reshape(ROWS)


def solution(mesh):
    in_specs = (P(("src", "own"), None), P(("src", "own")))
    out_specs = P(("src", "own"))
    return jax.shard_map(shards, mesh=mesh, in_specs=in_specs, out_specs=out_specs, check_vma=False)
```

```python
import functools
import math

import jax
import jax.numpy as jnp
from jax import lax
from jax.experimental import pallas as pl
from jax.experimental.pallas import tpu as pltpu
from jax.sharding import PartitionSpec as P

MESH = pl.DeviceIdType.MESH
F32, BF16, I32 = jnp.float32, jnp.bfloat16, jnp.int32

D = 1024
ROWS = 192
CAP = 12
OWNERS = 32
SLOTS = 64
CL_OWN = 32
QUARTERS = 4
QW = D // QUARTERS
BLK = QUARTERS * CAP
GRP = 16
NGRP = SLOTS // GRP
GROWS = GRP * CAP
HROWS = SLOTS * CAP
HALF = HROWS // 2
RETW = 256


def home_of(owner):
    return lax.rem(owner, 4), lax.rem(owner // 4, 4), (owner // 16) * 2


def gray(v):
    return v + (v // 2) * (1 - 2 * lax.rem(v, 2))


def at(x, y, z, core):
    return x, y * 8 + z * 2 + core


def div12(v):
    return (v * 5462) >> 16


def dot_nn(a, b):
    return lax.dot_general(a, b, (((1,), (0,)), ((), ())), preferred_element_type=F32)


def dot_nt(a, b):
    return lax.dot_general(a, b, (((1,), (1,)), ((), ())), preferred_element_type=F32)


def dot_tn(a, b):
    return lax.dot_general(a, b, (((0,), (0,)), ((), ())), preferred_element_type=F32)


def iota(shape, dim):
    return lax.broadcasted_iota(I32, shape, dim)


def swap_matrix():
    i, j = iota((GROWS, GROWS), 0), iota((GROWS, GROWS), 1)
    ab = div12(i)
    a, b = ab >> 2, ab & 3
    return (j == b * BLK + a * CAP + (i - ab * CAP)).astype(BF16)


def kernel(
    emb_hbm, ids_hbm, out_ref,
    emb_ref, ids_ref, send, meta_send, recv, meta_recv, rows, theirs, meta_theirs, id_col, best, back,
    emb_sem, ids_sem, send_sem, meta_send_sem, recv_sem, meta_recv_sem, pass_sem, theirs_sem,
    meta_pass_sem, meta_theirs_sem, back_send_sem, back_sem,
):
    src, own = lax.axis_index("src"), lax.axis_index("own")
    y, z, core = own // 8, lax.rem(own // 2, 4), lax.rem(own, 2)
    is_home, shard = lax.rem(z, 2) == 0, (z // 2) * 16 + y * 4 + src
    is_relay = (lax.rem(z, 2) == 1) & (core == 1)
    seat = y * 4 + src
    partner = (src, own + 1 - 2 * core)

    barrier = pltpu.get_barrier_semaphore()
    fetch = pltpu.make_async_copy(emb_hbm, emb_ref, emb_sem)
    fetch_ids = pltpu.make_async_copy(ids_hbm, ids_ref, ids_sem)
    fetch_ids.start()
    fetch.start()

    @pl.when(is_home)
    def _():
        pl.semaphore_signal(barrier, inc=1, device_id=partner, device_id_type=MESH)

        def greet(i, carry):
            to = lax.rem(z * 16 + seat + i, SLOTS)
            device = at(lax.rem(to, 4), lax.rem(to // 4, 4), to // 16, core)
            pl.semaphore_signal(barrier, inc=1, device_id=device, device_id_type=MESH)
            return carry

        lax.fori_loop(1, SLOTS, greet, 0)

    @pl.when(is_relay)
    def _():
        def greet(i, carry):
            device = at(lax.rem(i, 4), i // 4, lax.rem(z + 1, 4), core)
            pl.semaphore_signal(barrier, inc=1, device_id=device, device_id_type=MESH)
            return carry

        lax.fori_loop(0, GRP, greet, 0)

    fetch_ids.wait()
    ids = ids_ref[...]
    owner = ids >> 5
    onehot = iota((OWNERS, ROWS), 0) == owner
    onehot_b = onehot.astype(BF16)
    upto = (iota((ROWS, ROWS), 0) <= iota((ROWS, ROWS), 1)).astype(BF16)
    counts = dot_nn(onehot_b, upto)
    rank = jnp.sum(jnp.where(onehot, counts, 0.0), axis=0, keepdims=True).astype(I32) - 1
    place = owner * CAP + rank
    pick = (iota((OWNERS * CAP, ROWS), 0) == place).astype(BF16)

    local = (ids - owner * CL_OWN + 1).astype(F32)
    by_rank = jnp.where(iota((128, ROWS), 0) == rank, local, 0.0).astype(BF16)
    meta_send[...] = (dot_nt(onehot_b, by_rank) - 1.0).reshape(OWNERS, 1, 128)

    fetch.wait()
    values = emb_ref[...].astype(F32)
    mean = jnp.sum(values * values, axis=1, keepdims=True) * (1.0 / D)
    scale = lax.rsqrt(mean + 1e-06) * (1.0 / math.sqrt(D))
    unit = (values * scale).astype(BF16)
    packed = dot_nn(pick, unit).astype(BF16)
    swap = swap_matrix()
    for k in range(OWNERS // 4):
        part = packed[k * BLK : (k + 1) * BLK]
        stacked = jnp.concatenate([part[:, q * QW : (q + 1) * QW] for q in range(QUARTERS)], axis=0)
        send[pl.ds(4 * k, 4)] = dot_nn(swap, stacked).astype(BF16).reshape(4, BLK, QW)

    @pl.when(is_home & (core == 1))
    def _():
        pl.semaphore_wait(barrier, OWNERS + GRP)

    @pl.when(jnp.logical_not(is_home & (core == 1)))
    def _():
        pl.semaphore_wait(barrier, OWNERS)

    plane = lax.rem(z // 2 + core, 2)

    def send_one(source, landed, device, sent, arrived, here):
        def away():
            pltpu.make_async_remote_copy(
                source, landed, sent, arrived, device_id=device, device_id_type=MESH
            ).start()

        if here is None:
            away()
        else:
            pl.when(jnp.logical_not(here))(away)
            pl.when(here)(lambda: pltpu.make_async_copy(source, landed, arrived).start())

    def half(p):
        hz = 2 * lax.rem(plane + p, 2)
        above = lax.rem(z - hz + 4, 4)
        group = gray(above)
        via = core * (above // 2) * (1 - lax.rem(above, 2))
        landing = seat + GRP * group * (1 - via)
        signal = group + via * (y - group)

        def place(j):
            if isinstance(j, int):
                dx, dy = (0, 1, 3, 2)[j % 4], (0, 1, 3, 2)[j // 4]
            else:
                dx, dy = gray(lax.rem(j, 4)), gray(j // 4)
            hx, hy = lax.rem(src + dx, 4), lax.rem(y + dy, 4)
            here = (above == 0) if isinstance(j, int) and j == 0 else None
            return hx, hy, 8 * hz + 4 * hy + hx, here

        def give(j, carry):
            hx, hy, to, here = place(j)
            send_one(
                send.at[to], recv.at[landing], at(hx, hy, hz + via, core), send_sem, recv_sem.at[signal], here
            )
            return carry

        def give_meta(j, carry):
            hx, hy, to, here = place(j)
            send_one(
                meta_send.at[to], meta_recv.at[GRP * group + seat], at(hx, hy, hz, core),
                meta_send_sem, meta_recv_sem, here,
            )
            return carry

        return give, give_meta

    def run(f, first, last):
        if first == 0:
            f(0, 0)
        lax.fori_loop(max(first, 1), last, f, 0, unroll=False)

    rows_a, ids_a = half(0)
    rows_b, ids_b = half(1)
    run(rows_a, 0, 8)
    run(ids_a, 0, GRP)
    run(ids_b, 0, GRP)
    run(rows_a, 8, GRP)
    run(rows_b, 0, GRP)

    def onward(k):
        return pltpu.make_async_remote_copy(
            recv.at[pl.ds(4 * k, 4)], recv.at[pl.ds(3 * GRP + 4 * k, 4)], pass_sem, recv_sem.at[3],
            device_id=at(src, y, z - 1, core), device_id_type=MESH,
        )

    @pl.when(is_relay)
    def _():
        for k in range(4):
            block = recv.at[pl.ds(4 * k, 4)]
            pltpu.make_async_copy(block, block, recv_sem.at[k]).wait()
            onward(k).start()

    @pl.when(is_home)
    def _():
        lane_of = iota((GRP, GROWS), 1)
        spread = (div12(lane_of) == iota((GRP, GROWS), 0)).astype(BF16)
        nth_row = iota((GRP, GROWS), 0) == lane_of - div12(lane_of) * CAP
        sub = iota((GROWS, 128), 0)
        nth_col = iota((GROWS, 128), 1) == sub - div12(sub) * CAP

        pltpu.make_async_copy(meta_recv, meta_recv, meta_recv_sem).wait()
        meta_pass = pltpu.make_async_remote_copy(
            meta_recv, meta_theirs, meta_pass_sem, meta_theirs_sem,
            device_id=partner, device_id_type=MESH,
        )
        meta_pass.start()

        def down(ref, g):
            ids_g = ref[pl.ds(g * GRP, GRP)].reshape(GRP, 128).astype(BF16)
            wide = dot_tn(spread, ids_g)
            return ids_g, jnp.sum(jnp.where(nth_col, wide, 0.0), axis=1, keepdims=True)

        along = []
        for g in range(NGRP):
            ids_g, col_g = down(meta_recv, g)
            id_col[0, g * GROWS : (g + 1) * GROWS] = col_g
            wide = dot_tn(ids_g, spread)[:GRP]
            along.append(jnp.sum(jnp.where(nth_row, wide, 0.0), axis=0, keepdims=True))
        along = jnp.concatenate(along, axis=1)
        meta_pass.wait_recv()
        for g in range(NGRP):
            id_col[1, g * GROWS : (g + 1) * GROWS] = down(meta_theirs, g)[1]

        def passing(g):
            part = pl.ds(g * GROWS, GROWS)
            return pltpu.make_async_remote_copy(
                rows.at[part], theirs.at[part], pass_sem, theirs_sem.at[g // 2],
                device_id=partner, device_id_type=MESH,
            )

        def turn(g):
            block = recv.at[pl.ds(g * GRP, GRP)]
            pltpu.make_async_copy(block, block, recv_sem.at[g]).wait()
            for k in range(GRP // 4):
                four = recv[pl.ds(g * GRP + 4 * k, 4)].reshape(GROWS, QW)
                turned = dot_nn(swap, four).astype(BF16)
                first = g * GROWS + k * BLK
                for q in range(QUARTERS):
                    rows[first : first + BLK, q * QW : (q + 1) * QW] = turned[q * BLK : (q + 1) * BLK]
            passing(g).start()

        def top(ref, side, down_at, along_at):
            mine = rows[along_at : along_at + HALF, :]
            scores = dot_nt(ref[down_at : down_at + HALF, :], mine)
            keep = id_col[side, down_at : down_at + HALF] == along[:, along_at : along_at + HALF]
            if side == 0 and down_at == along_at:
                keep &= iota((HALF, HALF), 0) != iota((HALF, HALF), 1)
            return jnp.max(jnp.where(keep, scores, -1.0), axis=0, keepdims=True)

        def arrived(half):
            part = theirs.at[pl.ds(half * HALF, HALF)]
            pltpu.make_async_copy(part, part, theirs_sem.at[half]).wait()

        def give_back(g, found):
            best[g, :, :GROWS] = found
            for to in range(GRP):
                device = at(to % 4, to // 4, lax.rem(z + (0, 1, 3, 2)[g], 4), core)

                def one(device=device):
                    pltpu.make_async_remote_copy(
                        best.at[g], back.at[shard], back_send_sem, back_sem,
                        device_id=device, device_id_type=MESH,
                    ).start()

                if g:
                    one()
                else:
                    pl.when(to != seat)(one)
            if g == 0:
                pltpu.make_async_copy(best.at[0], back.at[shard], back_sem).start()

        turn(0)
        turn(1)
        first = top(rows, 0, 0, 0)
        arrived(0)
        first = jnp.maximum(first, top(theirs, 1, 0, 0))
        turn(2)
        turn(3)
        second = jnp.maximum(top(rows, 0, 0, HALF), top(rows, 0, HALF, HALF))
        second = jnp.maximum(second, top(theirs, 1, 0, HALF))
        first = jnp.maximum(first, top(rows, 0, HALF, 0))
        arrived(1)
        second = jnp.maximum(jnp.maximum(second, top(theirs, 1, HALF, HALF)), -1.0)
        give_back(3, second[:, GROWS:])
        give_back(2, second[:, :GROWS])
        first = jnp.maximum(jnp.maximum(first, top(theirs, 1, HALF, 0)), -1.0)
        give_back(1, first[:, GROWS:])
        give_back(0, first[:, :GROWS])

    pltpu.make_async_copy(back, back, back_sem).wait()
    got = back[...].reshape(OWNERS, RETW)
    high = got.astype(BF16)
    rest = got - high.astype(F32)
    mid = rest.astype(BF16)
    low = (rest - mid.astype(F32)).astype(BF16)
    parts = jnp.concatenate([low, mid, high], axis=0)
    wide = dot_tn(parts, jnp.concatenate([onehot_b] * 3, axis=0))
    lane = seat * CAP + rank
    out_ref[...] = jnp.sum(jnp.where(iota((RETW, ROWS), 0) == lane, wide, 0.0), axis=0, keepdims=True)

    @pl.when(is_home)
    def _():
        part = send.at[pl.ds(0, OWNERS - 1)]
        pltpu.make_async_copy(part, part, send_sem).wait()
        part = meta_send.at[pl.ds(0, OWNERS - 1)]
        pltpu.make_async_copy(part, part, meta_send_sem).wait()
        pltpu.make_async_copy(meta_recv, meta_recv, meta_pass_sem).wait()
        pltpu.make_async_copy(rows, rows, pass_sem).wait()
        pltpu.make_async_copy(back, back, back_send_sem).wait()
        part = back.at[pl.ds(0, OWNERS - 1)]
        pltpu.make_async_copy(part, part, back_send_sem).wait()

    @pl.when(jnp.logical_not(is_home))
    def _():
        pltpu.make_async_copy(send, send, send_sem).wait()
        pltpu.make_async_copy(meta_send, meta_send, meta_send_sem).wait()

    @pl.when(is_relay)
    def _():
        part = recv.at[pl.ds(0, GRP)]
        pltpu.make_async_copy(part, part, pass_sem).wait()


def shards(embeddings, cluster_ids):
    dma = pltpu.SemaphoreType.DMA
    out = pl.pallas_call(
        kernel,
        out_shape=jax.ShapeDtypeStruct((1, ROWS), F32),
        in_specs=[pl.BlockSpec(memory_space=pltpu.HBM)] * 2,
        out_specs=pl.BlockSpec(memory_space=pltpu.VMEM),
        scratch_shapes=[
            pltpu.VMEM((ROWS, D), BF16),
            pltpu.VMEM((1, ROWS), I32),
            pltpu.VMEM((OWNERS, BLK, QW), BF16),
            pltpu.VMEM((OWNERS, 1, 128), F32),
            pltpu.VMEM((SLOTS, BLK, QW), BF16),
            pltpu.VMEM((SLOTS, 1, 128), F32),
            pltpu.VMEM((HROWS, D), BF16),
            pltpu.VMEM((HROWS, D), BF16),
            pltpu.VMEM((SLOTS, 1, 128), F32),
            pltpu.VMEM((2, HROWS, 1), F32),
            pltpu.VMEM((NGRP, 1, RETW), F32),
            pltpu.VMEM((OWNERS, 1, RETW), F32),
            dma, dma, dma, dma, dma((NGRP,)), dma, dma, dma((2,)), dma, dma, dma, dma,
        ],
        compiler_params=pltpu.CompilerParams(
            collective_id=0, has_side_effects=True, vmem_limit_bytes=60 << 20
        ),
    )(embeddings, cluster_ids.reshape(1, ROWS))
    return out.reshape(ROWS)


def solution(mesh):
    in_specs = (P(("src", "own"), None), P(("src", "own")))
    out_specs = P(("src", "own"))
    return jax.shard_map(shards, mesh=mesh, in_specs=in_specs, out_specs=out_specs, check_vma=False)
```
